32 devices in a mesh: dp: 8 (over z, y), tensor: 4 (over x, core).
Axes of the slice: x: 2, y: 2, z: 4, core: 2. Of those that a mesh axis runs over, the one named last changes fastest.
Arguments:
- tokens: bfloat16 [8192, 768], P(('dp', 'tensor')), may hold values from -6 to 6
- lengths: int32 [8, 2], P('dp'), may hold values from 256 to 768, as said below
- w_qkv: bfloat16 [768, 3, 768], P('dp', None, 'tensor'), may hold values from -0.21875 to 0.21875
- w_attn_out: bfloat16 [768, 768], P('tensor', 'dp'), may hold values from -0.625 to 0.625
- w_in: bfloat16 [768, 2, 1152], P('dp', None, 'tensor'), may hold values from -0.21875 to 0.21875
- w_mlp_out: bfloat16 [1152, 768], P('tensor', 'dp'), may hold values from -0.1875 to 0.1875
- gain_attn: bfloat16 [768], P('dp'), may hold values from 0.5 to 1.5
- gain_mlp: bfloat16 [768], P('dp'), may hold values from 0.5 to 1.5
- cotangent: bfloat16 [8192, 768], P(('dp', 'tensor')), may hold values from -6 to 6
Outputs:
- output: bfloat16 [8192, 768], P(('dp', 'tensor'))
- grad_tokens: bfloat16 [8192, 768], P(('dp', 'tensor'))
- grad_qkv: float32 [768, 3, 768], P('dp', None, 'tensor')
- grad_attn_out: float32 [768, 768], P('tensor', 'dp')
- grad_in: float32 [768, 2, 1152], P('dp', None, 'tensor')
- grad_mlp_out: float32 [1152, 768], P('tensor', 'dp')
- grad_gain_attn: float32 [768], P('dp')
- grad_gain_mlp: float32 [768], P('dp')
The draws below stay inside these ranges and needn't reach their ends.
Inputs may be any that keep to these rules, and one draw needn't show every extreme that they name: Each row gives the lengths of the two sequences packed in order at the start of one group's 1024 slots; their sum lies above 768 and at most 1024, and in every draw some group's two lengths are 256 and 768.
All inputs are finite; a program needn't handle non-finite values.
Results may differ from the reference program's by a relative error of at most 0.02.
Values may be sent and summed in bfloat16 or wider, within the bound.
A program may use at most 128 MiB of HBM per device.

```python
import jax
import jax.numpy as jnp
from jax import lax

D = 768
FF = 1152
HEAD_DIM = 64
WINDOW = 128
MIN_LEN = 256
CAP = 1024
GROUPS = 8
TOKENS = 8192


def draw_lengths(key, part):
    key = jax.random.fold_in(key, 7)
    pad_key, split_key, pick_key = jax.random.split(key, 3)
    padding = jax.random.randint(pad_key, (GROUPS,), 0, CAP // 4, dtype=jnp.int32)
    filled = CAP - padding
    first_len = jax.random.randint(split_key, (GROUPS,), MIN_LEN, filled - MIN_LEN + 1, dtype=jnp.int32)
    chosen = jax.random.randint(pick_key, (), 0, GROUPS, dtype=jnp.int32)
    group_ids = jnp.arange(GROUPS, dtype=jnp.int32)
    second_len = jnp.where(group_ids == chosen, CAP - MIN_LEN, filled - first_len)
    first_len = jnp.where(group_ids == chosen, MIN_LEN, first_len)
    return jnp.stack([first_len, second_len], axis=1).astype(jnp.int32)


def levels(rng, shape, pieces, smallest, high):
    level, own = 1.0, jax.random.fold_in(rng, 6)
    for dim, parts in pieces:
        steps = jnp.exp(jax.random.uniform(jax.random.fold_in(own, dim), (parts,), jnp.float32, smallest / len(pieces), high / len(pieces)))
        level = level * jnp.repeat(steps, shape[dim] // parts).reshape([-1 if axis == dim else 1 for axis in range(len(shape))])
    return level


def bell_draw(key, dims, scale, limit, cuts=(), kind=jnp.bfloat16):
    level = levels(key, dims, cuts, -0.22, 0.18) if cuts else 1.0
    values = jax.random.normal(key, dims, jnp.float32) * scale * level
    return jnp.minimum(jnp.maximum(values, -limit), limit).astype(kind)


def setup_inputs(seed: int = 0) -> dict:
    streams_of = jax.random.split(jax.random.key(seed), 10)
    return {
        "tokens": bell_draw(streams_of[0], (TOKENS, D), 1.0, 6.0, ((0, 32),)),
        "lengths": draw_lengths(jax.random.fold_in(streams_of[9], 71), 0),
        "w_qkv": bell_draw(streams_of[2], (D, 3, D), D ** -0.5, 0.21875, ((0, 8), (2, 4))),
        "w_attn_out": bell_draw(streams_of[3], (D, D), (D // 8) ** -0.5, 0.625, ((0, 4), (1, 8))),
        "w_in": bell_draw(streams_of[4], (D, 2, FF), D ** -0.5, 0.21875, ((0, 8), (2, 4))),
        "w_mlp_out": bell_draw(streams_of[5], (FF, D), FF ** -0.5, 0.1875, ((0, 4), (1, 8))),
        "gain_attn": jnp.clip(1.0 + 0.1 * jax.random.normal(streams_of[6], (D,), jnp.float32), 0.5, 1.5).astype(jnp.bfloat16),
        "gain_mlp": jnp.clip(1.0 + 0.1 * jax.random.normal(streams_of[7], (D,), jnp.float32), 0.5, 1.5).astype(jnp.bfloat16),
        "cotangent": bell_draw(streams_of[8], (TOKENS, D), 1.0, 6.0, ((0, 32),)),
    }


NORM_EPS = 1e-05
ROPE_BASE = 10000.0
MASKED = -1e+30
HIGHEST = lax.Precision.HIGHEST

@jax.custom_vjp
def low(v):
    return lax.optimization_barrier(v.astype(jnp.bfloat16)).astype(jnp.float32)

@jax.custom_vjp
def low_back(v):
    return v

def low_keep(v):
    return (low(v), None)

def low_pass(kept, grad):
    return (grad,)

def back_keep(v):
    return (v, None)

def back_low(kept, grad):
    return (low(grad),)
low.defvjp(low_keep, low_pass)
low_back.defvjp(back_keep, back_low)

def hot_dot(left_mat, right_mat):
    return jnp.dot(left_mat, right_mat, precision=HIGHEST)

def norm_rows(values, gain):
    centre = values - lax.optimization_barrier(jnp.mean(values, axis=-1, keepdims=True))
    spread = lax.optimization_barrier(jnp.mean(centre * centre, axis=-1, keepdims=True))
    return centre * lax.rsqrt(spread + NORM_EPS) * gain

def run_layout(seq_pair, slot_count):
    slot_ids = jnp.arange(slot_count, dtype=jnp.int32)
    first_end = seq_pair[0].astype(jnp.int32)
    second_end = (seq_pair[0] + seq_pair[1]).astype(jnp.int32)
    run_ids = (slot_ids >= first_end).astype(jnp.int32) + (slot_ids >= second_end).astype(jnp.int32)
    run_start = jnp.where(run_ids == 0, 0, jnp.where(run_ids == 1, first_end, second_end)).astype(jnp.int32)
    return (run_ids, slot_ids - run_start)

def rope_tables(position, head_dim):
    half_dim = head_dim // 2
    inv_freq = ROPE_BASE ** (-(jnp.arange(half_dim, dtype=jnp.float32) * 2.0) / head_dim)
    angles = position.astype(jnp.float32)[:, None] * inv_freq[None, :]
    return (jnp.cos(angles)[:, None, :], jnp.sin(angles)[:, None, :])

def rotate(values, cos_tab, sin_tab):
    half_dim = values.shape[-1] // 2
    front_half = values[..., :half_dim]
    back_half = values[..., half_dim:]
    return jnp.concatenate([front_half * cos_tab - back_half * sin_tab, back_half * cos_tab + front_half * sin_tab], axis=-1)

def window_allowed(run_ids, run_pad, first_row, block_rows, half_win):
    row_runs = lax.dynamic_slice_in_dim(run_ids, first_row, block_rows, 0)
    key_runs = lax.dynamic_slice_in_dim(run_pad, first_row, block_rows + 2 * half_win, 0)
    offsets = jnp.arange(block_rows, dtype=jnp.int32)[:, None] + half_win - jnp.arange(block_rows + 2 * half_win, dtype=jnp.int32)[None, :]
    return (row_runs[:, None] == key_runs[None, :]) & (jnp.abs(offsets) <= half_win)

def attend(query_rot, key_rot, value_low, run_ids):
    slot_count = query_rot.shape[0]
    block_rows = min(512, slot_count)
    half_win = WINDOW // 2
    score_scale = HEAD_DIM ** (-0.5)
    key_pad = jnp.pad(key_rot, ((half_win, half_win), (0, 0), (0, 0)))
    value_pad = jnp.pad(value_low, ((half_win, half_win), (0, 0), (0, 0)))
    run_pad = jnp.pad(run_ids, (half_win, half_win), constant_values=-1)

    def one_block(block_index):
        first_row = block_index * block_rows
        q_blk = lax.dynamic_slice_in_dim(query_rot, first_row, block_rows, 0)
        k_blk = lax.dynamic_slice_in_dim(key_pad, first_row, block_rows + 2 * half_win, 0)
        v_blk = lax.dynamic_slice_in_dim(value_pad, first_row, block_rows + 2 * half_win, 0)
        allowed = window_allowed(run_ids, run_pad, first_row, block_rows, half_win)
        scores = low_back(jnp.einsum('ihc,jhc->hij', q_blk, k_blk, precision=HIGHEST) * score_scale)
        scores = jnp.where(allowed[None], scores, MASKED)
        row_max = lax.optimization_barrier(jnp.max(scores, axis=-1, keepdims=True))
        exp_scores = jnp.exp(scores - row_max)
        attn_prob = low(exp_scores / lax.optimization_barrier(jnp.sum(exp_scores, axis=-1, keepdims=True)))
        return jnp.einsum('hij,jhc->ihc', attn_prob, v_blk, precision=HIGHEST)
    block_outs = lax.map(jax.checkpoint(one_block), jnp.arange(slot_count // block_rows, dtype=jnp.int32))
    return block_outs.reshape(query_rot.shape)

def group_layer(tokens_f, seq_pair, qkv_f, attn_out_f, in_f, mlp_out_f, gain_one, gain_two):
    slot_count = tokens_f.shape[0]
    run_ids, position = run_layout(seq_pair, slot_count)
    cos_tab, sin_tab = rope_tables(position, HEAD_DIM)
    normed_one = low(norm_rows(tokens_f, gain_one))
    proj = low_back(hot_dot(normed_one, qkv_f.reshape(D, 3 * D))).reshape(slot_count, 3, D // HEAD_DIM, HEAD_DIM)
    query_rot = low(rotate(proj[:, 0], cos_tab, sin_tab))
    key_rot = low(rotate(proj[:, 1], cos_tab, sin_tab))
    value_low = low(proj[:, 2])
    attended = low(low_back(attend(query_rot, key_rot, value_low, run_ids))).reshape(slot_count, D)
    hidden = tokens_f + low_back(hot_dot(attended, attn_out_f))
    normed_two = low(norm_rows(hidden, gain_two))
    mixed_proj = low_back(hot_dot(normed_two, in_f.reshape(D, 2 * FF))).reshape(slot_count, 2, FF)
    gated_act = low(jax.nn.gelu(mixed_proj[:, 0], approximate=False) * mixed_proj[:, 1])
    return hidden + low_back(hot_dot(gated_act, mlp_out_f))

def reference(tokens, lengths, w_qkv, w_attn_out, w_in, w_mlp_out, gain_attn, gain_mlp, cotangent):

    def forward(tokens_f, qkv_f, attn_out_f, in_f, mlp_out_f, gain_one, gain_two):

        def per_group(group_args):
            return group_layer(group_args[0], group_args[1], qkv_f, attn_out_f, in_f, mlp_out_f, gain_one, gain_two)
        grouped = lax.map(jax.checkpoint(per_group), (tokens_f.reshape(GROUPS, CAP, D), lengths))
        return grouped.reshape(GROUPS * CAP, D)
    result, pull_back = jax.vjp(forward, tokens.astype(jnp.float32), w_qkv.astype(jnp.float32), w_attn_out.astype(jnp.float32), w_in.astype(jnp.float32), w_mlp_out.astype(jnp.float32), gain_attn.astype(jnp.float32), gain_mlp.astype(jnp.float32))
    grads = pull_back(cotangent.astype(jnp.float32))
    return (result.astype(jnp.bfloat16), grads[0].astype(jnp.bfloat16), grads[1], grads[2], grads[3], grads[4], grads[5], grads[6])
```

```python
import functools

import jax
import jax.numpy as jnp
from jax import lax
from jax.experimental import pallas as pl
from jax.experimental.pallas import tpu as pltpu
from jax.sharding import PartitionSpec as P

HEAD_DIM = 64
WINDOW = 128
NORM_EPS = 1e-05
ROPE_BASE = 10000.0
MASKED = -1e30
MESH = pl.DeviceIdType.MESH
BF = jnp.bfloat16
F32 = jnp.float32
NT = (((1,), (1,)), ((), ()))
VMEM = pl.BlockSpec(memory_space=pltpu.VMEM)
ANY = pl.BlockSpec(memory_space=pl.ANY)


def normal_rows(values):
    centre = values - jnp.mean(values, axis=-1, keepdims=True)
    spread = jnp.mean(centre * centre, axis=-1, keepdims=True)
    inv = lax.rsqrt(spread + NORM_EPS)
    return centre * inv, inv


def normal_back(values, grad):
    xhat, inv = normal_rows(values)
    mean_g = jnp.mean(grad, axis=-1, keepdims=True)
    mean_gx = jnp.mean(grad * xhat, axis=-1, keepdims=True)
    return inv * (grad - mean_g - xhat * mean_gx)


def remote(src, dst, send, recv, dev):
    return pltpu.make_async_remote_copy(
        src_ref=src, dst_ref=dst, send_sem=send, recv_sem=recv, device_id=dev, device_id_type=MESH
    )


def tensor_place():
    dp, t = lax.axis_index("dp"), lax.axis_index("tensor")
    x, core = lax.div(t, 2), lax.rem(t, 2)
    return dp, t, x, core, x * 2 + 1 - core, (1 - x) * 2 + core


def dp_place(dp_size):
    dp, t = lax.axis_index("dp"), lax.axis_index("tensor")
    return dp, t, lax.div(dp, 2), lax.rem(dp, 2), dp_size // 2


def greet(devices):
    barrier = pltpu.get_barrier_semaphore()
    for dev in devices:
        pl.semaphore_signal(barrier, inc=1, device_id=dev, device_id_type=MESH)
    pl.semaphore_wait(barrier, len(devices))


def tensor_peers():
    dp, t, x, core, corep, xp = tensor_place()
    return [(dp, corep), (dp, xp)]


def dp_peers(dp_size):
    dp, t, hi, lo, high = dp_place(dp_size)
    return [(hi * 2 + 1 - lo, t)] + [(lax.rem(hi + k, high) * 2 + lo, t) for k in range(1, high)]


class Gather:
    def __init__(self, src, out, sems):
        dp, t, x, core, corep, xp = tensor_place()
        send, recv, here = sems
        self.own = pltpu.make_async_copy(src, out.at[t], here)
        self.over_x = remote(src, out.at[t], send.at[0], recv.at[0], (dp, xp))
        self.to_core = remote(src, out.at[t], send.at[1], recv.at[1], (dp, corep))
        self.relay = remote(out.at[xp], out.at[xp], send.at[2], recv.at[2], (dp, corep))

    def start(self):
        self.over_x.start()
        self.to_core.start()
        self.own.start()

    def forward(self):
        self.over_x.wait_recv()
        self.relay.start()

    def finish(self):
        self.to_core.wait_recv()
        self.relay.wait_recv()
        self.over_x.wait_send()
        self.to_core.wait_send()
        self.relay.wait_send()
        self.own.wait()


GATHER_SEMS = [pltpu.SemaphoreType.DMA((3,)), pltpu.SemaphoreType.DMA((3,)), pltpu.SemaphoreType.DMA]


def scatter_sum(part, scratch):
    sbuf, r1, pbuf, r2, send, recv = scratch
    dp, t, x, core, corep, xp = tensor_place()
    far = remote(sbuf.at[0], r1.at[0], send.at[0], recv.at[0], (dp, corep))
    near = remote(sbuf.at[1], r1.at[1], send.at[1], recv.at[1], (dp, corep))
    over = remote(pbuf, r2, send.at[2], recv.at[2], (dp, xp))
    sbuf[0] = part((1 - x) * 2 + 1 - core).astype(BF)
    far.start()
    mine = part(xp)
    far.wait_recv()
    pbuf[...] = (mine + r1[0].astype(F32)).astype(BF)
    over.start()
    sbuf[1] = part(corep).astype(BF)
    near.start()
    total = part(t)
    near.wait_recv()
    total = total + r1[1].astype(F32)
    over.wait_recv()
    total = total + r2[...].astype(F32)
    far.wait_send()
    near.wait_send()
    over.wait_send()
    return total


def scatter_scratch(rows, width):
    return [
        pltpu.VMEM((2, rows, width), BF),
        pltpu.VMEM((2, rows, width), BF),
        pltpu.VMEM((rows, width), BF),
        pltpu.VMEM((rows, width), BF),
        pltpu.SemaphoreType.DMA((3,)),
        pltpu.SemaphoreType.DMA((3,)),
    ]


def params(ident):
    return pltpu.CompilerParams(
        collective_id=ident, has_side_effects=True, vmem_limit_bytes=48 * 1024 * 1024
    )


def first_kernel(dp_size, tok, cot, slab, xfull, cfull, wfull, xhat, *scr):
    gx, gc = Gather(xhat, xfull, scr[0:3]), Gather(cot, cfull, scr[3:6])
    zsend, zrecv, ysend, yrecv, here = scr[6:]
    dp, t, hi, lo, high = dp_place(dp_size)
    ypeer = (hi * 2 + 1 - lo, t)
    greet(tensor_peers() + dp_peers(dp_size))
    mine = pltpu.make_async_copy(slab, wfull.at[dp], here)
    ycopies = [remote(slab, wfull.at[dp], ysend.at[0], yrecv.at[0], ypeer)]
    zcopies = []
    for k in range(1, high):
        peer = (lax.rem(hi + k, high) * 2 + lo, t)
        zcopies.append(remote(slab, wfull.at[dp], zsend.at[k], zrecv.at[k], peer))
        block = lax.rem(hi - k + high, high) * 2 + lo
        ycopies.append(remote(wfull.at[block], wfull.at[block], ysend.at[k], yrecv.at[k], ypeer))
    ycopies[0].start()
    for copy in zcopies:
        copy.start()
    mine.start()
    xhat[...] = normal_rows(tok[...].astype(F32))[0].astype(BF)
    gx.start()
    gc.start()
    gx.forward()
    gc.forward()
    for k in range(1, high):
        zcopies[k - 1].wait_recv()
        ycopies[k].start()
    gx.finish()
    gc.finish()
    for copy in ycopies:
        copy.wait_recv()
    for copy in ycopies + zcopies:
        copy.wait_send()
    mine.wait()


def hidden_kernel(att, wo, tok, hid, x2full, xhat, *scr):
    rows = tok.shape[0]
    greet(tensor_peers())

    def part(b):
        lhs = att[pl.ds(pl.multiple_of(b * rows, rows), rows), :]
        return lax.dot_general(lhs, wo[...], NT, preferred_element_type=F32)

    hidden = tok[...].astype(F32) + scatter_sum(part, scr[3:9])
    hid[...] = hidden
    xhat[...] = normal_rows(hidden)[0].astype(BF)
    gather = Gather(xhat, x2full, scr[0:3])
    gather.start()
    gather.forward()
    gather.finish()


def middle_kernel(gated, wm, dmix, win, hid, cot, out, dhid, dbfull, dbr, *scr):
    rows = hid.shape[0]
    greet(tensor_peers())

    def part_of(lhs_ref, w_ref):
        def part(b):
            lhs = lhs_ref[pl.ds(pl.multiple_of(b * rows, rows), rows), :]
            return lax.dot_general(lhs, w_ref[...], NT, preferred_element_type=F32)

        return part

    grad = scatter_sum(part_of(dmix, win), scr[3:9])
    d_hidden = cot[...].astype(F32) + normal_back(hid[...], grad)
    dhid[...] = d_hidden
    dbr[...] = d_hidden.astype(BF)
    gather = Gather(dbr, dbfull, scr[0:3])
    gather.start()
    gather.forward()
    out[...] = (hid[...] + scatter_sum(part_of(gated, wm), scr[9:15])).astype(BF)
    gather.finish()


def last_kernel(dp_size, dproj, wqkv, tok, dhid, grads, gtok, gsum, ry, zs, zr, *scr):
    rows = tok.shape[0]
    ysend, yrecv, zsend, zrecv = scr[6:]
    dp, t, hi, lo, high = dp_place(dp_size)
    ypeer = (hi * 2 + 1 - lo, t)
    greet(tensor_peers() + dp_peers(dp_size))
    ycopies = []
    zcopies = []
    order = list(range(1, high)) + [0]
    for k in range(high):
        block_hi = lax.rem(hi + k, high)
        ycopies.append(
            remote(grads.at[block_hi * 2 + 1 - lo], ry.at[k], ysend.at[k], yrecv.at[k], ypeer)
        )
        zcopies.append(
            remote(zs.at[k], zr.at[k], zsend.at[k], zrecv.at[k], (block_hi * 2 + lo, t))
        )
    for k in order:
        ycopies[k].start()

    def part(b):
        lhs = dproj[pl.ds(pl.multiple_of(b * rows, rows), rows), :]
        return lax.dot_general(lhs, wqkv[...], NT, preferred_element_type=F32)

    grad = scatter_sum(part, scr[0:6])
    gtok[...] = (dhid[...] + normal_back(tok[...].astype(F32), grad)).astype(BF)
    for k in range(1, high):
        ycopies[k].wait_recv()
        block = lax.rem(hi + k, high) * 2 + lo
        zs[k] = (grads[block].astype(F32) + ry[k].astype(F32)).astype(BF)
        zcopies[k].start()
    ycopies[0].wait_recv()
    total = grads[hi * 2 + lo].astype(F32) + ry[0].astype(F32)
    for k in range(1, high):
        zcopies[k].wait_recv()
        total = total + zr[k].astype(F32)
    gsum[...] = total
    for copy in ycopies + zcopies[1:]:
        copy.wait_send()


def run_layout(seq_pair, slot_count):
    slot_ids = jnp.arange(slot_count, dtype=jnp.int32)
    first_end = seq_pair[0]
    second_end = seq_pair[0] + seq_pair[1]
    run_ids = (slot_ids >= first_end).astype(jnp.int32) + (slot_ids >= second_end).astype(jnp.int32)
    run_start = jnp.where(run_ids == 0, 0, jnp.where(run_ids == 1, first_end, second_end))
    return (run_ids, slot_ids - run_start)


def rope_tables(position, head_dim):
    half_dim = head_dim // 2
    inv_freq = ROPE_BASE ** (-(jnp.arange(half_dim, dtype=jnp.float32) * 2.0) / head_dim)
    angles = position.astype(jnp.float32)[:, None] * inv_freq[None, :]
    return (jnp.cos(angles)[:, None, :], jnp.sin(angles)[:, None, :])


def rotate(values, cos_tab, sin_tab):
    half_dim = values.shape[-1] // 2
    front_half = values[..., :half_dim]
    back_half = values[..., half_dim:]
    return jnp.concatenate(
        [front_half * cos_tab - back_half * sin_tab, back_half * cos_tab + front_half * sin_tab],
        axis=-1,
    )


def unrotate(values, cos_tab, sin_tab):
    half_dim = values.shape[-1] // 2
    front_half = values[..., :half_dim]
    back_half = values[..., half_dim:]
    return jnp.concatenate(
        [front_half * cos_tab + back_half * sin_tab, back_half * cos_tab - front_half * sin_tab],
        axis=-1,
    )


def window_allowed(run_ids, run_pad, first_row, block_rows, half_win):
    row_runs = lax.dynamic_slice_in_dim(run_ids, first_row, block_rows, 0)
    key_runs = lax.dynamic_slice_in_dim(run_pad, first_row, block_rows + 2 * half_win, 0)
    offsets = (
        jnp.arange(block_rows, dtype=jnp.int32)[:, None]
        + half_win
        - jnp.arange(block_rows + 2 * half_win, dtype=jnp.int32)[None, :]
    )
    return (row_runs[:, None] == key_runs[None, :]) & (jnp.abs(offsets) <= half_win)


def padded_inputs(key_rot, value_low, run_ids, half_win):
    key_pad = jnp.pad(key_rot, ((half_win, half_win), (0, 0), (0, 0)))
    value_pad = jnp.pad(value_low, ((half_win, half_win), (0, 0), (0, 0)))
    run_pad = jnp.pad(run_ids, (half_win, half_win), constant_values=-1)
    return (key_pad, value_pad, run_pad)


def block_scores(q_blk, k_blk, allowed, score_scale):
    scores = (
        jnp.einsum("ihc,jhc->hij", q_blk, k_blk, preferred_element_type=jnp.float32) * score_scale
    )
    return jnp.where(allowed[None], scores, MASKED)


def attend_forward(query_rot, key_rot, value_low, run_ids):
    slot_count, heads_here, head_dim = query_rot.shape
    block_rows = min(512, slot_count)
    half_win = WINDOW // 2
    key_width = block_rows + 2 * half_win
    score_scale = head_dim ** (-0.5)
    key_pad, value_pad, run_pad = padded_inputs(key_rot, value_low, run_ids, half_win)

    def one_block(block_index):
        first_row = block_index * block_rows
        q_blk = lax.dynamic_slice_in_dim(query_rot, first_row, block_rows, 0)
        k_blk = lax.dynamic_slice_in_dim(key_pad, first_row, key_width, 0)
        v_blk = lax.dynamic_slice_in_dim(value_pad, first_row, key_width, 0)
        allowed = window_allowed(run_ids, run_pad, first_row, block_rows, half_win)
        scores = block_scores(q_blk, k_blk, allowed, score_scale)
        row_max = jnp.max(scores, axis=-1, keepdims=True)
        exp_total = jnp.sum(jnp.exp(scores - row_max), axis=-1, keepdims=True)
        log_total = row_max + jnp.log(exp_total)
        attn_prob = jnp.exp(scores - log_total).astype(jnp.bfloat16)
        block_out = jnp.einsum("hij,jhc->ihc", attn_prob, v_blk, preferred_element_type=jnp.float32)
        return (block_out.astype(jnp.bfloat16), log_total)

    block_outs, log_totals = lax.map(
        one_block, jnp.arange(slot_count // block_rows, dtype=jnp.int32)
    )
    return (block_outs.reshape(slot_count, heads_here, head_dim), log_totals)


def attend_backward(query_rot, key_rot, value_low, run_ids, log_totals, grad_attended):
    slot_count, heads_here, head_dim = query_rot.shape
    block_rows = min(512, slot_count)
    half_win = WINDOW // 2
    key_width = block_rows + 2 * half_win
    score_scale = head_dim ** (-0.5)
    key_pad, value_pad, run_pad = padded_inputs(key_rot, value_low, run_ids, half_win)

    def one_block(carry, inputs):
        grad_key_pad, grad_value_pad = carry
        block_index, log_total = inputs
        first_row = block_index * block_rows
        q_blk = lax.dynamic_slice_in_dim(query_rot, first_row, block_rows, 0)
        k_blk = lax.dynamic_slice_in_dim(key_pad, first_row, key_width, 0)
        v_blk = lax.dynamic_slice_in_dim(value_pad, first_row, key_width, 0)
        g_blk = lax.dynamic_slice_in_dim(grad_attended, first_row, block_rows, 0)
        allowed = window_allowed(run_ids, run_pad, first_row, block_rows, half_win)
        scores = block_scores(q_blk, k_blk, allowed, score_scale)
        attn_prob = jnp.exp(scores - log_total)
        prob_low = attn_prob.astype(jnp.bfloat16)
        grad_v = jnp.einsum("hij,ihc->jhc", prob_low, g_blk, preferred_element_type=jnp.float32)
        grad_p = jnp.einsum("ihc,jhc->hij", g_blk, v_blk, preferred_element_type=jnp.float32)
        row_inner = jnp.sum(attn_prob * grad_p, axis=-1, keepdims=True)
        grad_s = (attn_prob * (grad_p - row_inner)).astype(jnp.bfloat16)
        grad_q = (
            jnp.einsum("hij,jhc->ihc", grad_s, k_blk, preferred_element_type=jnp.float32)
            * score_scale
        )
        grad_k = (
            jnp.einsum("hij,ihc->jhc", grad_s, q_blk, preferred_element_type=jnp.float32)
            * score_scale
        )
        key_part = lax.dynamic_slice_in_dim(grad_key_pad, first_row, key_width, 0) + grad_k
        value_part = lax.dynamic_slice_in_dim(grad_value_pad, first_row, key_width, 0) + grad_v
        grad_key_pad = lax.dynamic_update_slice_in_dim(grad_key_pad, key_part, first_row, 0)
        grad_value_pad = lax.dynamic_update_slice_in_dim(grad_value_pad, value_part, first_row, 0)
        return ((grad_key_pad, grad_value_pad), grad_q)

    zero_grads = jnp.zeros((slot_count + 2 * half_win, heads_here, head_dim), jnp.float32)
    block_ids = jnp.arange(slot_count // block_rows, dtype=jnp.int32)
    (grad_key_pad, grad_value_pad), grad_query = lax.scan(
        one_block, (zero_grads, zero_grads), (block_ids, log_totals)
    )
    grad_query = grad_query.reshape(slot_count, heads_here, head_dim)
    return (
        grad_query,
        grad_key_pad[half_win : half_win + slot_count],
        grad_value_pad[half_win : half_win + slot_count],
    )


def attention_forward(xfull, wqkv, lengths, nq):
    slots = xfull.shape[0]
    heads = nq // HEAD_DIM
    run_ids, position = run_layout(lengths[0], slots)
    cos_tab, sin_tab = rope_tables(position, HEAD_DIM)
    proj = jnp.dot(xfull, wqkv, preferred_element_type=F32).reshape(slots, 3, heads, HEAD_DIM)
    query = rotate(proj[:, 0], cos_tab, sin_tab).astype(BF)
    key = rotate(proj[:, 1], cos_tab, sin_tab).astype(BF)
    value = proj[:, 2].astype(BF)
    attended, log_totals = attend_forward(query, key, value, run_ids)
    return (query, key, value, log_totals, run_ids, cos_tab, sin_tab), attended.reshape(slots, nq)


def attention_backward(saved, d_attended, lengths, nq):
    query, key, value, log_totals, run_ids, cos_tab, sin_tab = saved
    slots = query.shape[0]
    dq, dk, dv = attend_backward(
        query, key, value, run_ids, log_totals, d_attended.reshape(query.shape)
    )
    d_proj = jnp.stack(
        [unrotate(dq, cos_tab, sin_tab), unrotate(dk, cos_tab, sin_tab), dv], axis=1
    )
    return d_proj.astype(BF).reshape(slots, 3 * nq)


def on_device(tokens, lengths, w_qkv, w_attn_out, w_in, w_mlp_out, gain_attn, gain_mlp, cotangent):
    dp_size, tensor_size = lax.axis_size("dp"), lax.axis_size("tensor")
    rows, width = tokens.shape
    own = w_qkv.shape[0]
    slots = rows * tensor_size
    nq, nf = w_qkv.shape[2], w_in.shape[2]
    c_attn, c_in, c_mlp, c_all = 3 * nq, 4 * nq, 4 * nq + 2 * nf, 4 * nq + 3 * nf
    gain_one = gain_attn.astype(F32)[:, None]
    gain_two = gain_mlp.astype(F32)[:, None]
    qkv_own = w_qkv.reshape(own, 3 * nq).astype(F32)
    in_own = w_in.reshape(own, 2 * nf).astype(F32)
    slab = jnp.concatenate(
        [
            (qkv_own * gain_one).astype(BF),
            w_attn_out.T,
            (in_own * gain_two).astype(BF),
            w_mlp_out.T,
        ],
        axis=1,
    )
    full = jax.ShapeDtypeStruct((tensor_size, rows, width), BF)
    half = dp_size // 2
    xfull, cfull, wfull = pl.pallas_call(
        functools.partial(first_kernel, dp_size),
        out_shape=(full, full, jax.ShapeDtypeStruct((dp_size, own, c_all), BF)),
        in_specs=[VMEM, VMEM, ANY],
        out_specs=(ANY, ANY, ANY),
        scratch_shapes=[pltpu.VMEM((rows, width), BF)]
        + GATHER_SEMS * 2
        + [pltpu.SemaphoreType.DMA((half,))] * 4
        + [pltpu.SemaphoreType.DMA],
        compiler_params=params(0),
    )(tokens, cotangent, slab)
    xfull = xfull.reshape(slots, width)
    cfull = cfull.reshape(slots, width)
    wfull = wfull.reshape(width, c_all)
    wqkv, wo = wfull[:, :c_attn], wfull[:, c_attn:c_in]
    win, wm = wfull[:, c_in:c_mlp], wfull[:, c_mlp:]

    saved, attended = attention_forward(xfull, wqkv, lengths, nq)

    hid, x2full = pl.pallas_call(
        hidden_kernel,
        out_shape=(jax.ShapeDtypeStruct((rows, width), F32), full),
        in_specs=[VMEM] * 3,
        out_specs=(VMEM, ANY),
        scratch_shapes=[pltpu.VMEM((rows, width), BF)] + GATHER_SEMS + scatter_scratch(rows, width),
        compiler_params=params(1),
    )(attended, wo, tokens)
    x2full = x2full.reshape(slots, width)

    mixed = jnp.dot(x2full, win, preferred_element_type=F32)
    d_gated = jnp.dot(cfull, wm, preferred_element_type=F32)

    def gate(inputs, gates):
        return jax.nn.gelu(inputs, approximate=False) * gates

    gated_f, pull = jax.vjp(gate, mixed[:, :nf], mixed[:, nf:])
    gated = gated_f.astype(BF)
    d_mixed = jnp.concatenate(pull(d_gated), axis=1).astype(BF)

    output, dhid, dbfull = pl.pallas_call(
        middle_kernel,
        out_shape=(
            jax.ShapeDtypeStruct((rows, width), BF),
            jax.ShapeDtypeStruct((rows, width), F32),
            full,
        ),
        in_specs=[VMEM] * 6,
        out_specs=(VMEM, VMEM, ANY),
        scratch_shapes=[pltpu.VMEM((rows, width), BF)]
        + GATHER_SEMS
        + scatter_scratch(rows, width) * 2,
        compiler_params=params(2),
    )(gated, wm, d_mixed, win, hid, cotangent)
    dbfull = dbfull.reshape(slots, width)

    d_attended = jnp.dot(dbfull, wo, preferred_element_type=F32).astype(BF)
    d_proj = attention_backward(saved, d_attended, lengths, nq)

    def over_rows(left, right):
        return lax.dot_general(
            left, right, (((0,), (0,)), ((), ())), preferred_element_type=F32
        ).astype(BF)

    grads = jnp.concatenate(
        [
            over_rows(xfull, d_proj),
            over_rows(dbfull, attended),
            over_rows(x2full, d_mixed),
            over_rows(cfull, gated),
        ],
        axis=1,
    ).reshape(dp_size, own, c_all)
    block = pltpu.VMEM((half, own, c_all), BF)
    grad_tokens, gsum = pl.pallas_call(
        functools.partial(last_kernel, dp_size),
        out_shape=(
            jax.ShapeDtypeStruct((rows, width), BF),
            jax.ShapeDtypeStruct((own, c_all), F32),
        ),
        in_specs=[VMEM] * 5,
        out_specs=(VMEM, VMEM),
        scratch_shapes=[block] * 3
        + scatter_scratch(rows, width)
        + [pltpu.SemaphoreType.DMA((half,))] * 4,
        compiler_params=params(3),
    )(d_proj, wqkv, tokens, dhid, grads)

    sum_qkv, sum_in = gsum[:, :c_attn], gsum[:, c_in:c_mlp]
    gain_grads = lax.psum(
        jnp.stack([jnp.sum(sum_qkv * qkv_own, axis=1), jnp.sum(sum_in * in_own, axis=1)]), "tensor"
    )
    return (
        output,
        grad_tokens,
        (sum_qkv * gain_one).reshape(own, 3, nq),
        gsum[:, c_attn:c_in].T,
        (sum_in * gain_two).reshape(own, 2, nf),
        gsum[:, c_mlp:].T,
        gain_grads[0],
        gain_grads[1],
    )


def solution(mesh):
    return jax.shard_map(
        on_device,
        mesh=mesh,
        in_specs=(
            P(("dp", "tensor"), None),
            P("dp", None),
            P("dp", None, "tensor"),
            P("tensor", "dp"),
            P("dp", None, "tensor"),
            P("tensor", "dp"),
            P("dp"),
            P("dp"),
            P(("dp", "tensor"), None),
        ),
        out_specs=(
            P(("dp", "tensor"), None),
            P(("dp", "tensor"), None),
            P("dp", None, "tensor"),
            P("tensor", "dp"),
            P("dp", None, "tensor"),
            P("tensor", "dp"),
            P("dp"),
            P("dp"),
        ),
        check_vma=False,
    )
```

```python
import functools

import jax
import jax.numpy as jnp
from jax import lax
from jax.experimental import pallas as pl
from jax.experimental.pallas import tpu as pltpu
from jax.sharding import PartitionSpec as P

HEAD_DIM = 64
WINDOW = 128
NORM_EPS = 1e-05
ROPE_BASE = 10000.0
MASKED = -1e30
MESH = pl.DeviceIdType.MESH
BF = jnp.bfloat16
F32 = jnp.float32
NT = (((1,), (1,)), ((), ()))
VMEM = pl.BlockSpec(memory_space=pltpu.VMEM)
ANY = pl.BlockSpec(memory_space=pl.ANY)


def normal_rows(values):
    centre = values - jnp.mean(values, axis=-1, keepdims=True)
    spread = jnp.mean(centre * centre, axis=-1, keepdims=True)
    inv = lax.rsqrt(spread + NORM_EPS)
    return centre * inv, inv


def normal_back(values, grad):
    xhat, inv = normal_rows(values)
    mean_g = jnp.mean(grad, axis=-1, keepdims=True)
    mean_gx = jnp.mean(grad * xhat, axis=-1, keepdims=True)
    return inv * (grad - mean_g - xhat * mean_gx)


def remote(src, dst, send, recv, dev):
    return pltpu.make_async_remote_copy(
        src_ref=src, dst_ref=dst, send_sem=send, recv_sem=recv, device_id=dev, device_id_type=MESH
    )


def tensor_place():
    dp, t = lax.axis_index("dp"), lax.axis_index("tensor")
    x, core = lax.div(t, 2), lax.rem(t, 2)
    return dp, t, x, core, x * 2 + 1 - core, (1 - x) * 2 + core


def dp_place(dp_size):
    dp, t = lax.axis_index("dp"), lax.axis_index("tensor")
    return dp, t, lax.div(dp, 2), lax.rem(dp, 2), dp_size // 2


def greet(devices):
    barrier = pltpu.get_barrier_semaphore()
    for dev in devices:
        pl.semaphore_signal(barrier, inc=1, device_id=dev, device_id_type=MESH)
    pl.semaphore_wait(barrier, len(devices))


def tensor_peers():
    dp, t, x, core, corep, xp = tensor_place()
    return [(dp, corep), (dp, xp)]


def dp_peers(dp_size):
    dp, t, hi, lo, high = dp_place(dp_size)
    return [(hi * 2 + 1 - lo, t)] + [(lax.rem(hi + k, high) * 2 + lo, t) for k in range(1, high)]


class Gather:
    def __init__(self, src, out, sems):
        dp, t, x, core, corep, xp = tensor_place()
        send, recv, here = sems
        self.own = pltpu.make_async_copy(src, out.at[t], here)
        self.over_x = remote(src, out.at[t], send.at[0], recv.at[0], (dp, xp))
        self.to_core = remote(src, out.at[t], send.at[1], recv.at[1], (dp, corep))
        self.relay = remote(out.at[xp], out.at[xp], send.at[2], recv.at[2], (dp, corep))

    def start(self):
        self.over_x.start()
        self.to_core.start()
        self.own.start()

    def forward(self):
        self.over_x.wait_recv()
        self.relay.start()

    def finish(self):
        self.to_core.wait_recv()
        self.relay.wait_recv()
        self.over_x.wait_send()
        self.to_core.wait_send()
        self.relay.wait_send()
        self.own.wait()


GATHER_SEMS = [pltpu.SemaphoreType.DMA((3,)), pltpu.SemaphoreType.DMA((3,)), pltpu.SemaphoreType.DMA]


def scatter_sum(part, scratch):
    sbuf, r1, pbuf, r2, send, recv = scratch
    dp, t, x, core, corep, xp = tensor_place()
    far = remote(sbuf.at[0], r1.at[0], send.at[0], recv.at[0], (dp, corep))
    near = remote(sbuf.at[1], r1.at[1], send.at[1], recv.at[1], (dp, corep))
    over = remote(pbuf, r2, send.at[2], recv.at[2], (dp, xp))
    sbuf[0] = part((1 - x) * 2 + 1 - core).astype(BF)
    far.start()
    mine = part(xp)
    far.wait_recv()
    pbuf[...] = (mine + r1[0].astype(F32)).astype(BF)
    over.start()
    sbuf[1] = part(corep).astype(BF)
    near.start()
    total = part(t)
    near.wait_recv()
    total = total + r1[1].astype(F32)
    over.wait_recv()
    total = total + r2[...].astype(F32)
    far.wait_send()
    near.wait_send()
    over.wait_send()
    return total


def scatter_scratch(rows, width):
    return [
        pltpu.VMEM((2, rows, width), BF),
        pltpu.VMEM((2, rows, width), BF),
        pltpu.VMEM((rows, width), BF),
        pltpu.VMEM((rows, width), BF),
        pltpu.SemaphoreType.DMA((3,)),
        pltpu.SemaphoreType.DMA((3,)),
    ]


def params(ident):
    return pltpu.CompilerParams(
        collective_id=ident, has_side_effects=True, vmem_limit_bytes=48 * 1024 * 1024
    )


def first_kernel(dp_size, tok, cot, slab, xfull, cfull, wfull, xhat, *scr):
    gx, gc = Gather(xhat, xfull, scr[0:3]), Gather(cot, cfull, scr[3:6])
    zsend, zrecv, ysend, yrecv, here = scr[6:]
    dp, t, hi, lo, high = dp_place(dp_size)
    ypeer = (hi * 2 + 1 - lo, t)
    greet(tensor_peers() + dp_peers(dp_size))
    mine = pltpu.make_async_copy(slab, wfull.at[dp], here)
    ycopies = [remote(slab, wfull.at[dp], ysend.at[0], yrecv.at[0], ypeer)]
    zcopies = []
    for k in range(1, high):
        peer = (lax.rem(hi + k, high) * 2 + lo, t)
        zcopies.append(remote(slab, wfull.at[dp], zsend.at[k], zrecv.at[k], peer))
        block = lax.rem(hi - k + high, high) * 2 + lo
        ycopies.append(remote(wfull.at[block], wfull.at[block], ysend.at[k], yrecv.at[k], ypeer))
    ycopies[0].start()
    for copy in zcopies:
        copy.start()
    mine.start()
    xhat[...] = normal_rows(tok[...].astype(F32))[0].astype(BF)
    gx.start()
    gc.start()
    gx.forward()
    gc.forward()
    for k in range(1, high):
        zcopies[k - 1].wait_recv()
        ycopies[k].start()
    gx.finish()
    gc.finish()
    for copy in ycopies:
        copy.wait_recv()
    for copy in ycopies + zcopies:
        copy.wait_send()
    mine.wait()


def hidden_kernel(c_attn, c_in, att, w, tok, hid, x2full, xhat, *scr):
    rows = tok.shape[0]
    greet(tensor_peers())

    def part(b):
        lhs = att[pl.ds(pl.multiple_of(b * rows, rows), rows), :]
        return lax.dot_general(lhs, w[:, c_attn:c_in], NT, preferred_element_type=F32)

    hidden = tok[...].astype(F32) + scatter_sum(part, scr[3:9])
    hid[...] = hidden
    xhat[...] = normal_rows(hidden)[0].astype(BF)
    gather = Gather(xhat, x2full, scr[0:3])
    gather.start()
    gather.forward()
    gather.finish()


def middle_kernel(c_in, c_mlp, gated, w, dmix, hid, cot, out, dhid, dbfull, dbr, *scr):
    rows = hid.shape[0]
    greet(tensor_peers())

    def part_of(lhs_ref, low, high):
        def part(b):
            lhs = lhs_ref[pl.ds(pl.multiple_of(b * rows, rows), rows), :]
            return lax.dot_general(lhs, w[:, low:high], NT, preferred_element_type=F32)

        return part

    grad = scatter_sum(part_of(dmix, c_in, c_mlp), scr[3:9])
    d_hidden = cot[...].astype(F32) + normal_back(hid[...], grad)
    dhid[...] = d_hidden
    dbr[...] = d_hidden.astype(BF)
    gather = Gather(dbr, dbfull, scr[0:3])
    gather.start()
    gather.forward()
    out[...] = (hid[...] + scatter_sum(part_of(gated, c_mlp, w.shape[1]), scr[9:15])).astype(BF)
    gather.finish()


def last_kernel(dp_size, c_attn, dproj, w, tok, dhid, grads, gtok, gsum, ry, zs, zr, *scr):
    rows = tok.shape[0]
    ysend, yrecv, zsend, zrecv = scr[6:]
    dp, t, hi, lo, high = dp_place(dp_size)
    ypeer = (hi * 2 + 1 - lo, t)
    greet(tensor_peers() + dp_peers(dp_size))
    ycopies = []
    zcopies = []
    order = list(range(1, high)) + [0]
    for k in range(high):
        block_hi = lax.rem(hi + k, high)
        ycopies.append(
            remote(grads.at[block_hi * 2 + 1 - lo], ry.at[k], ysend.at[k], yrecv.at[k], ypeer)
        )
        zcopies.append(
            remote(zs.at[k], zr.at[k], zsend.at[k], zrecv.at[k], (block_hi * 2 + lo, t))
        )
    for k in order:
        ycopies[k].start()

    def part(b):
        lhs = dproj[pl.ds(pl.multiple_of(b * rows, rows), rows), :]
        return lax.dot_general(lhs, w[:, :c_attn], NT, preferred_element_type=F32)

    grad = scatter_sum(part, scr[0:6])
    gtok[...] = (dhid[...] + normal_back(tok[...].astype(F32), grad)).astype(BF)
    for k in range(1, high):
        ycopies[k].wait_recv()
        block = lax.rem(hi + k, high) * 2 + lo
        zs[k] = (grads[block].astype(F32) + ry[k].astype(F32)).astype(BF)
        zcopies[k].start()
    ycopies[0].wait_recv()
    total = grads[hi * 2 + lo].astype(F32) + ry[0].astype(F32)
    for k in range(1, high):
        zcopies[k].wait_recv()
        total = total + zr[k].astype(F32)
    gsum[...] = total
    for copy in ycopies + zcopies[1:]:
        copy.wait_send()


BLOCK = 128
SPAN = BLOCK + WINDOW
NN = (((1,), (0,)), ((), ()))
TN = (((0,), (0,)), ((), ()))


def mat(left, right, dims):
    return lax.dot_general(left, right, dims, preferred_element_type=F32)


def rope_tables(lengths, slots):
    slot_ids = jnp.arange(slots, dtype=jnp.int32)
    first_end, second_end = lengths[0, 0], lengths[0, 0] + lengths[0, 1]
    start = jnp.where(
        slot_ids < first_end, 0, jnp.where(slot_ids < second_end, first_end, second_end)
    )
    lane = jnp.arange(2 * HEAD_DIM, dtype=jnp.int32) % HEAD_DIM
    half = HEAD_DIM // 2
    inv_freq = ROPE_BASE ** (-((lane % half).astype(F32) * 2.0) / HEAD_DIM)
    angles = (slot_ids - start).astype(F32)[:, None] * inv_freq[None, :]
    return jnp.cos(angles), jnp.sin(angles) * jnp.where(lane < half, -1.0, 1.0)[None, :]


def swap_halves(values):
    half = HEAD_DIM // 2
    lane = lax.broadcasted_iota(jnp.int32, values.shape, 1)
    ahead = pltpu.roll(values, 2 * HEAD_DIM - half, 1)
    behind = pltpu.roll(values, half, 1)
    return jnp.where(lax.rem(lane, HEAD_DIM) < half, ahead, behind)


def allowed_pairs(lens, first, start):
    row = first + lax.broadcasted_iota(jnp.int32, (BLOCK, SPAN), 0)
    col = start + lax.broadcasted_iota(jnp.int32, (BLOCK, SPAN), 1)
    one, two = lens[0, 0], lens[0, 0] + lens[0, 1]
    ids = lambda v: (v >= one).astype(jnp.int32) + (v >= two).astype(jnp.int32)
    return (ids(row) == ids(col)) & (jnp.abs(row - col) <= WINDOW // 2)


def blocks_of(slots):
    for first in range(0, slots, BLOCK):
        yield first, min(max(first - WINDOW // 2, 0), slots - SPAN)


def softmax_block(q, k, allowed):
    scores = jnp.where(allowed, mat(q, k, NT) * HEAD_DIM ** (-0.5), MASKED)
    grown = jnp.exp(scores - jnp.max(scores, axis=-1, keepdims=True))
    return grown * (1.0 / jnp.sum(grown, axis=-1, keepdims=True))


def forward_kernel(nq, lens, xfull, w, cos, sin, qkv, att):
    slots = xfull.shape[0]
    proj = mat(xfull[...], w[:, : 3 * nq], NN)
    for at in range(0, 2 * nq, 128):
        piece = proj[:, at : at + 128]
        qkv[:, at : at + 128] = (piece * cos[...] + swap_halves(piece) * sin[...]).astype(BF)
    qkv[:, 2 * nq :] = proj[:, 2 * nq :].astype(BF)
    for first, start in blocks_of(slots):
        allowed = allowed_pairs(lens, first, start)
        for h in range(0, nq, HEAD_DIM):
            q = qkv[first : first + BLOCK, h : h + HEAD_DIM]
            k = qkv[start : start + SPAN, nq + h : nq + h + HEAD_DIM]
            v = qkv[start : start + SPAN, 2 * nq + h : 2 * nq + h + HEAD_DIM]
            probs = softmax_block(q, k, allowed).astype(BF)
            att[first : first + BLOCK, h : h + HEAD_DIM] = mat(probs, v, NN).astype(BF)


def backward_kernel(
    nq, nf, lens, qkv, dbfull, att, w, cos, sin, xfull, x2full, cfull, dmix, gated,
    dproj, grads, dqk, dv, datt,
):
    slots = xfull.shape[0]
    scale = HEAD_DIM ** (-0.5)
    datt[...] = mat(dbfull[...], w[:, 3 * nq : 4 * nq], NN).astype(BF)
    dqk[:, nq:] = jnp.zeros((slots, nq), F32)
    dv[...] = jnp.zeros((slots, nq), F32)
    for first, start in blocks_of(slots):
        allowed = allowed_pairs(lens, first, start)
        here, there = slice(first, first + BLOCK), slice(start, start + SPAN)
        for h in range(0, nq, HEAD_DIM):
            q = qkv[here, h : h + HEAD_DIM]
            k = qkv[there, nq + h : nq + h + HEAD_DIM]
            v = qkv[there, 2 * nq + h : 2 * nq + h + HEAD_DIM]
            g = datt[here, h : h + HEAD_DIM]
            p = softmax_block(q, k, allowed)
            dp = mat(g, v, NT)
            inner = jnp.sum(p * dp, axis=-1, keepdims=True)
            ds = (p * (dp - inner)).astype(BF)
            dqk[here, h : h + HEAD_DIM] = mat(ds, k, NN) * scale
            dqk[there, nq + h : nq + h + HEAD_DIM] += mat(ds, q, TN) * scale
            dv[there, h : h + HEAD_DIM] += mat(p.astype(BF), g, TN)
    for at in range(0, 2 * nq, 128):
        piece = dqk[:, at : at + 128]
        dproj[:, at : at + 128] = (piece * cos[...] - swap_halves(piece) * sin[...]).astype(BF)
    dproj[:, 2 * nq :] = dv[...].astype(BF)
    c_attn, c_in, c_mlp = 3 * nq, 4 * nq, 4 * nq + 2 * nf
    grads[:, :c_attn] = mat(xfull[...], dproj[...], TN).astype(BF)
    grads[:, c_attn:c_in] = mat(dbfull[...], att[...], TN).astype(BF)
    grads[:, c_in:c_mlp] = mat(x2full[...], dmix[...], TN).astype(BF)
    grads[:, c_mlp:] = mat(cfull[...], gated[...], TN).astype(BF)


def on_device(tokens, lengths, w_qkv, w_attn_out, w_in, w_mlp_out, gain_attn, gain_mlp, cotangent):
    dp_size, tensor_size = lax.axis_size("dp"), lax.axis_size("tensor")
    rows, width = tokens.shape
    own = w_qkv.shape[0]
    slots = rows * tensor_size
    nq, nf = w_qkv.shape[2], w_in.shape[2]
    c_attn, c_in, c_mlp, c_all = 3 * nq, 4 * nq, 4 * nq + 2 * nf, 4 * nq + 3 * nf
    gain_one = gain_attn.astype(F32)[:, None]
    gain_two = gain_mlp.astype(F32)[:, None]
    qkv_own = w_qkv.reshape(own, 3 * nq).astype(F32)
    in_own = w_in.reshape(own, 2 * nf).astype(F32)
    slab = jnp.concatenate(
        [
            (qkv_own * gain_one).astype(BF),
            w_attn_out.T,
            (in_own * gain_two).astype(BF),
            w_mlp_out.T,
        ],
        axis=1,
    )
    full = jax.ShapeDtypeStruct((tensor_size, rows, width), BF)
    half = dp_size // 2
    xfull, cfull, wfull = pl.pallas_call(
        functools.partial(first_kernel, dp_size),
        out_shape=(full, full, jax.ShapeDtypeStruct((dp_size, own, c_all), BF)),
        in_specs=[VMEM, VMEM, ANY],
        out_specs=(ANY, ANY, ANY),
        scratch_shapes=[pltpu.VMEM((rows, width), BF)]
        + GATHER_SEMS * 2
        + [pltpu.SemaphoreType.DMA((half,))] * 4
        + [pltpu.SemaphoreType.DMA],
        compiler_params=params(0),
    )(tokens, cotangent, slab)
    xfull = xfull.reshape(slots, width)
    cfull = cfull.reshape(slots, width)
    wfull = wfull.reshape(width, c_all)
    win, wm = wfull[:, c_in:c_mlp], wfull[:, c_mlp:]

    cos_tab, sin_tab = rope_tables(lengths, slots)
    big = pltpu.CompilerParams(vmem_limit_bytes=56 * 1024 * 1024)
    smem = pl.BlockSpec(memory_space=pltpu.SMEM)
    qkv, attended = pl.pallas_call(
        functools.partial(forward_kernel, nq),
        out_shape=(
            jax.ShapeDtypeStruct((slots, 3 * nq), BF),
            jax.ShapeDtypeStruct((slots, nq), BF),
        ),
        in_specs=[smem] + [VMEM] * 4,
        out_specs=(VMEM, VMEM),
        compiler_params=big,
    )(lengths, xfull, wfull, cos_tab, sin_tab)

    hid, x2full = pl.pallas_call(
        functools.partial(hidden_kernel, c_attn, c_in),
        out_shape=(jax.ShapeDtypeStruct((rows, width), F32), full),
        in_specs=[VMEM] * 3,
        out_specs=(VMEM, ANY),
        scratch_shapes=[pltpu.VMEM((rows, width), BF)] + GATHER_SEMS + scatter_scratch(rows, width),
        compiler_params=params(1),
    )(attended, wfull, tokens)
    x2full = x2full.reshape(slots, width)

    mixed = jnp.dot(x2full, win, preferred_element_type=F32)
    d_gated = jnp.dot(cfull, wm, preferred_element_type=F32)

    def gate(inputs, gates):
        return jax.nn.gelu(inputs, approximate=False) * gates

    gated_f, pull = jax.vjp(gate, mixed[:, :nf], mixed[:, nf:])
    gated = gated_f.astype(BF)
    d_mixed = jnp.concatenate(pull(d_gated), axis=1).astype(BF)

    output, dhid, dbfull = pl.pallas_call(
        functools.partial(middle_kernel, c_in, c_mlp),
        out_shape=(
            jax.ShapeDtypeStruct((rows, width), BF),
            jax.ShapeDtypeStruct((rows, width), F32),
            full,
        ),
        in_specs=[VMEM] * 5,
        out_specs=(VMEM, VMEM, ANY),
        scratch_shapes=[pltpu.VMEM((rows, width), BF)]
        + GATHER_SEMS
        + scatter_scratch(rows, width) * 2,
        compiler_params=params(2),
    )(gated, wfull, d_mixed, hid, cotangent)
    dbfull = dbfull.reshape(slots, width)

    d_proj, grads = pl.pallas_call(
        functools.partial(backward_kernel, nq, nf),
        out_shape=(
            jax.ShapeDtypeStruct((slots, 3 * nq), BF),
            jax.ShapeDtypeStruct((width, c_all), BF),
        ),
        in_specs=[smem] + [VMEM] * 11,
        out_specs=(VMEM, VMEM),
        scratch_shapes=[
            pltpu.VMEM((slots, 2 * nq), F32),
            pltpu.VMEM((slots, nq), F32),
            pltpu.VMEM((slots, nq), BF),
        ],
        compiler_params=big,
    )(
        lengths, qkv, dbfull, attended, wfull, cos_tab, sin_tab, xfull, x2full, cfull,
        d_mixed, gated,
    )
    grads = grads.reshape(dp_size, own, c_all)
    block = pltpu.VMEM((half, own, c_all), BF)
    grad_tokens, gsum = pl.pallas_call(
        functools.partial(last_kernel, dp_size, c_attn),
        out_shape=(
            jax.ShapeDtypeStruct((rows, width), BF),
            jax.ShapeDtypeStruct((own, c_all), F32),
        ),
        in_specs=[VMEM] * 5,
        out_specs=(VMEM, VMEM),
        scratch_shapes=[block] * 3
        + scatter_scratch(rows, width)
        + [pltpu.SemaphoreType.DMA((half,))] * 4,
        compiler_params=params(3),
    )(d_proj, wfull, tokens, dhid, grads)

    sum_qkv, sum_in = gsum[:, :c_attn], gsum[:, c_in:c_mlp]
    gain_grads = lax.psum(
        jnp.stack([jnp.sum(sum_qkv * qkv_own, axis=1), jnp.sum(sum_in * in_own, axis=1)]), "tensor"
    )
    return (
        output,
        grad_tokens,
        (sum_qkv * gain_one).reshape(own, 3, nq),
        gsum[:, c_attn:c_in].T,
        (sum_in * gain_two).reshape(own, 2, nf),
        gsum[:, c_mlp:].T,
        gain_grads[0],
        gain_grads[1],
    )


def solution(mesh):
    return jax.shard_map(
        on_device,
        mesh=mesh,
        in_specs=(
            P(("dp", "tensor"), None),
            P("dp", None),
            P("dp", None, "tensor"),
            P("tensor", "dp"),
            P("dp", None, "tensor"),
            P("tensor", "dp"),
            P("dp"),
            P("dp"),
            P(("dp", "tensor"), None),
        ),
        out_specs=(
            P(("dp", "tensor"), None),
            P(("dp", "tensor"), None),
            P("dp", None, "tensor"),
            P("tensor", "dp"),
            P("dp", None, "tensor"),
            P("tensor", "dp"),
            P("dp"),
            P("dp"),
        ),
        check_vma=False,
    )
```

```python
import functools

import jax
import jax.numpy as jnp
from jax import lax
from jax.experimental import pallas as pl
from jax.experimental.pallas import tpu as pltpu
from jax.sharding import PartitionSpec as P

HEAD_DIM = 64
WINDOW = 128
NORM_EPS = 1e-05
ROPE_BASE = 10000.0
MASKED = -1e30
MESH = pl.DeviceIdType.MESH
BF = jnp.bfloat16
F32 = jnp.float32
NT = (((1,), (1,)), ((), ()))
VMEM = pl.BlockSpec(memory_space=pltpu.VMEM)
ANY = pl.BlockSpec(memory_space=pl.ANY)


def normal_rows(values):
    centre = values - jnp.mean(values, axis=-1, keepdims=True)
    spread = jnp.mean(centre * centre, axis=-1, keepdims=True)
    inv = lax.rsqrt(spread + NORM_EPS)
    return centre * inv, inv


def normal_back(values, grad):
    xhat, inv = normal_rows(values)
    mean_g = jnp.mean(grad, axis=-1, keepdims=True)
    mean_gx = jnp.mean(grad * xhat, axis=-1, keepdims=True)
    return inv * (grad - mean_g - xhat * mean_gx)


def remote(src, dst, send, recv, dev):
    return pltpu.make_async_remote_copy(
        src_ref=src, dst_ref=dst, send_sem=send, recv_sem=recv, device_id=dev, device_id_type=MESH
    )


def tensor_place():
    dp, t = lax.axis_index("dp"), lax.axis_index("tensor")
    x, core = lax.div(t, 2), lax.rem(t, 2)
    return dp, t, x, core, x * 2 + 1 - core, (1 - x) * 2 + core


def dp_place(dp_size):
    dp, t = lax.axis_index("dp"), lax.axis_index("tensor")
    return dp, t, lax.div(dp, 2), lax.rem(dp, 2), dp_size // 2


def greet(devices):
    barrier = pltpu.get_barrier_semaphore()
    for dev in devices:
        pl.semaphore_signal(barrier, inc=1, device_id=dev, device_id_type=MESH)
    pl.semaphore_wait(barrier, len(devices))


def tensor_peers():
    dp, t, x, core, corep, xp = tensor_place()
    return [(dp, corep), (dp, xp)]


def tensor_others(size):
    dp, t = lax.axis_index("dp"), lax.axis_index("tensor")
    return [(dp, lax.rem(t + k, size)) for k in range(1, size)]


def dp_peers(dp_size):
    dp, t, hi, lo, high = dp_place(dp_size)
    return [(hi * 2 + 1 - lo, t)] + [(lax.rem(hi + k, high) * 2 + lo, t) for k in range(1, high)]


class Gather:
    def __init__(self, src, out, sems):
        dp, t, x, core, corep, xp = tensor_place()
        send, recv, here = sems
        self.own = pltpu.make_async_copy(src, out.at[t], here)
        self.over_x = remote(src, out.at[t], send.at[0], recv.at[0], (dp, xp))
        self.to_core = remote(src, out.at[t], send.at[1], recv.at[1], (dp, corep))
        self.relay = remote(out.at[xp], out.at[xp], send.at[2], recv.at[2], (dp, corep))

    def start(self):
        self.over_x.start()
        self.to_core.start()
        self.own.start()

    def forward(self):
        self.over_x.wait_recv()
        self.relay.start()

    def finish(self):
        self.to_core.wait_recv()
        self.relay.wait_recv()
        self.over_x.wait_send()
        self.to_core.wait_send()
        self.relay.wait_send()
        self.own.wait()


GATHER_SEMS = [pltpu.SemaphoreType.DMA((3,)), pltpu.SemaphoreType.DMA((3,)), pltpu.SemaphoreType.DMA]


class ScatterSum:
    def __init__(self, part, scratch):
        self.part = part
        self.sbuf, self.r1, self.pbuf, self.r2, send, recv = scratch
        dp, t, x, core, corep, xp = tensor_place()
        self.place = (t, x, core, corep, xp)
        pair = (dp, corep)
        self.far = remote(self.sbuf.at[0], self.r1.at[0], send.at[0], recv.at[0], pair)
        self.near = remote(self.sbuf.at[1], self.r1.at[1], send.at[1], recv.at[1], pair)
        self.over = remote(self.pbuf, self.r2, send.at[2], recv.at[2], (dp, xp))

    def begin(self):
        t, x, core, corep, xp = self.place
        self.sbuf[0] = self.part((1 - x) * 2 + 1 - core).astype(BF)
        self.far.start()
        mine = self.part(xp)
        self.far.wait_recv()
        self.pbuf[...] = (mine + self.r1[0].astype(F32)).astype(BF)
        self.over.start()
        self.sbuf[1] = self.part(corep).astype(BF)
        self.near.start()

    def finish(self):
        total = self.part(self.place[0])
        self.near.wait_recv()
        total = total + self.r1[1].astype(F32)
        self.over.wait_recv()
        total = total + self.r2[...].astype(F32)
        for copy in (self.far, self.near, self.over):
            copy.wait_send()
        return total


class DpGather:
    def __init__(self, dp_size, slab, full, sems):
        zsend, zrecv, ysend, yrecv, here = sems
        dp, t, hi, lo, high = dp_place(dp_size)
        ypeer = (hi * 2 + 1 - lo, t)
        self.mine = pltpu.make_async_copy(slab, full.at[dp], here)
        self.ycopies = [remote(slab, full.at[dp], ysend.at[0], yrecv.at[0], ypeer)]
        self.zcopies = []
        for k in range(1, high):
            peer = (lax.rem(hi + k, high) * 2 + lo, t)
            self.zcopies.append(remote(slab, full.at[dp], zsend.at[k], zrecv.at[k], peer))
            block = lax.rem(hi - k + high, high) * 2 + lo
            self.ycopies.append(
                remote(full.at[block], full.at[block], ysend.at[k], yrecv.at[k], ypeer)
            )

    def start(self):
        self.ycopies[0].start()
        for copy in self.zcopies:
            copy.start()
        self.mine.start()

    def forward(self):
        for zcopy, ycopy in zip(self.zcopies, self.ycopies[1:]):
            zcopy.wait_recv()
            ycopy.start()

    def finish(self):
        for copy in self.ycopies:
            copy.wait_recv()
        for copy in self.ycopies + self.zcopies:
            copy.wait_send()
        self.mine.wait()


class DpScatter:
    def __init__(self, dp_size, grads, scratch):
        self.grads = grads
        self.ry, self.zs, self.zr, ysend, yrecv, zsend, zrecv = scratch
        dp, t, hi, lo, high = dp_place(dp_size)
        ypeer = (hi * 2 + 1 - lo, t)
        self.high = high
        self.ycopies, self.zcopies, self.blocks = [], [], []
        for k in range(high):
            block_hi = lax.rem(hi + k, high)
            self.blocks.append(block_hi * 2 + lo)
            self.ycopies.append(
                remote(
                    grads.at[block_hi * 2 + 1 - lo], self.ry.at[k], ysend.at[k], yrecv.at[k], ypeer
                )
            )
            if k:
                peer = (block_hi * 2 + lo, t)
                self.zcopies.append(
                    remote(self.zs.at[k], self.zr.at[k], zsend.at[k], zrecv.at[k], peer)
                )

    def start(self):
        for copy in self.ycopies[1:] + self.ycopies[:1]:
            copy.start()

    def forward(self):
        for k in range(1, self.high):
            self.ycopies[k].wait_recv()
            pair_sum = self.grads[self.blocks[k]].astype(F32) + self.ry[k].astype(F32)
            self.zs[k] = pair_sum.astype(BF)
            self.zcopies[k - 1].start()

    def finish(self):
        self.ycopies[0].wait_recv()
        total = self.grads[self.blocks[0]].astype(F32) + self.ry[0].astype(F32)
        for k in range(1, self.high):
            self.zcopies[k - 1].wait_recv()
            total = total + self.zr[k].astype(F32)
        for copy in self.ycopies + self.zcopies:
            copy.wait_send()
        return total


def dp_gather_sems(half):
    return [pltpu.SemaphoreType.DMA((half,))] * 4 + [pltpu.SemaphoreType.DMA]


def dp_scatter_scratch(half, own, width):
    return [pltpu.VMEM((half, own, width), BF)] * 3 + [pltpu.SemaphoreType.DMA((half,))] * 4


def scatter_scratch(rows, width):
    return [
        pltpu.VMEM((2, rows, width), BF),
        pltpu.VMEM((2, rows, width), BF),
        pltpu.VMEM((rows, width), BF),
        pltpu.VMEM((rows, width), BF),
        pltpu.SemaphoreType.DMA((3,)),
        pltpu.SemaphoreType.DMA((3,)),
    ]


def params(ident):
    return pltpu.CompilerParams(
        collective_id=ident, has_side_effects=True, vmem_limit_bytes=48 * 1024 * 1024
    )


def block_product(lhs_ref, w, low, high, rows):
    def part(b):
        lhs = lhs_ref[pl.ds(pl.multiple_of(b * rows, rows), rows), :]
        return lax.dot_general(lhs, w[:, low:high], NT, preferred_element_type=F32)

    return part


def first_kernel(dp_size, tok, cot, slab, xfull, cfull, wfull, xhat, *scr):
    gx, gc = Gather(xhat, xfull, scr[0:3]), Gather(cot, cfull, scr[3:6])
    weights = DpGather(dp_size, slab, wfull, scr[6:11])
    greet(tensor_peers() + dp_peers(dp_size))
    weights.start()
    xhat[...] = normal_rows(tok[...].astype(F32))[0].astype(BF)
    gx.start()
    gc.start()
    weights.forward()
    gx.forward()
    gc.forward()
    gx.finish()
    gc.finish()
    weights.finish()


def hidden_kernel(dp_size, c_attn, c_one, att, w, tok, slab, hid, x2full, w2full, xhat, *scr):
    rows = tok.shape[0]
    greet(tensor_peers() + dp_peers(dp_size))
    weights = DpGather(dp_size, slab, w2full, scr[9:14])
    weights.start()
    branch = ScatterSum(block_product(att, w, c_attn, c_one, rows), scr[3:9])
    branch.begin()
    hidden = tok[...].astype(F32) + branch.finish()
    hid[...] = hidden
    xhat[...] = normal_rows(hidden)[0].astype(BF)
    gather = Gather(xhat, x2full, scr[0:3])
    gather.start()
    weights.forward()
    gather.forward()
    gather.finish()
    weights.finish()


def middle_kernel(dp_size, c_in, dmix, w2, hid, cot, grads, dhid, dbfull, gsum, dbr, *scr):
    rows = hid.shape[0]
    greet(tensor_peers() + dp_peers(dp_size))
    weight_sum = DpScatter(dp_size, grads, scr[9:16])
    weight_sum.start()
    normed = ScatterSum(block_product(dmix, w2, 0, c_in, rows), scr[3:9])
    normed.begin()
    weight_sum.forward()
    d_hidden = cot[...].astype(F32) + normal_back(hid[...], normed.finish())
    dhid[...] = d_hidden
    dbr[...] = d_hidden.astype(BF)
    gather = Gather(dbr, dbfull, scr[0:3])
    gather.start()
    gather.forward()
    gsum[...] = weight_sum.finish()
    gather.finish()


def last_kernel(
    dp_size, t_size, c_attn, c_in, dproj, w, tok, dhid, grads, gated, w2, hid, raw_one, raw_two,
    gsum_two, gtok, out, gsum, gains, gbuf, grecv, gsend_sem, grecv_sem, *scr,
):
    rows = tok.shape[0]
    others = tensor_others(t_size)
    greet(others + dp_peers(dp_size))
    weight_sum = DpScatter(dp_size, grads, scr[12:19])
    weight_sum.start()
    normed = ScatterSum(block_product(dproj, w, 0, c_attn, rows), scr[0:6])
    result = ScatterSum(block_product(gated, w2, c_in, w2.shape[1], rows), scr[6:12])
    normed.begin()
    weight_sum.forward()
    result.begin()
    gtok[...] = (dhid[...] + normal_back(tok[...].astype(F32), normed.finish())).astype(BF)
    total = weight_sum.finish()
    gsum[...] = total
    gain_one = jnp.sum(total[:, :c_attn] * raw_one[...], axis=1, keepdims=True)
    gain_two = jnp.sum(gsum_two[:, :c_in] * raw_two[...], axis=1, keepdims=True)
    lane = lax.broadcasted_iota(jnp.int32, gbuf.shape, 1)
    gbuf[...] = jnp.where(lane < 64, gain_one, gain_two)
    copies = [
        remote(gbuf, grecv.at[k], gsend_sem.at[k], grecv_sem.at[k], peer)
        for k, peer in enumerate(others)
    ]
    for copy in copies:
        copy.start()
    out[...] = (hid[...] + result.finish()).astype(BF)
    gain_total = gbuf[...]
    for k, copy in enumerate(copies):
        copy.wait_recv()
        gain_total = gain_total + grecv[k]
    gains[...] = gain_total
    for copy in copies:
        copy.wait_send()


BLOCK = 128
SPAN = BLOCK + WINDOW
NN = (((1,), (0,)), ((), ()))
TN = (((0,), (0,)), ((), ()))


def mat(left, right, dims):
    return lax.dot_general(left, right, dims, preferred_element_type=F32)


def rope_tables(lengths, slots):
    slot_ids = jnp.arange(slots, dtype=jnp.int32)
    first_end, second_end = lengths[0, 0], lengths[0, 0] + lengths[0, 1]
    start = jnp.where(
        slot_ids < first_end, 0, jnp.where(slot_ids < second_end, first_end, second_end)
    )
    lane = jnp.arange(2 * HEAD_DIM, dtype=jnp.int32) % HEAD_DIM
    half = HEAD_DIM // 2
    inv_freq = ROPE_BASE ** (-((lane % half).astype(F32) * 2.0) / HEAD_DIM)
    angles = (slot_ids - start).astype(F32)[:, None] * inv_freq[None, :]
    return jnp.cos(angles), jnp.sin(angles) * jnp.where(lane < half, -1.0, 1.0)[None, :]


def swap_halves(values):
    half = HEAD_DIM // 2
    lane = lax.broadcasted_iota(jnp.int32, values.shape, 1)
    ahead = pltpu.roll(values, 2 * HEAD_DIM - half, 1)
    behind = pltpu.roll(values, half, 1)
    return jnp.where(lax.rem(lane, HEAD_DIM) < half, ahead, behind)


def allowed_pairs(lens, first, start):
    row = first + lax.broadcasted_iota(jnp.int32, (BLOCK, SPAN), 0)
    col = start + lax.broadcasted_iota(jnp.int32, (BLOCK, SPAN), 1)
    one, two = lens[0, 0], lens[0, 0] + lens[0, 1]
    ids = lambda v: (v >= one).astype(jnp.int32) + (v >= two).astype(jnp.int32)
    return (ids(row) == ids(col)) & (jnp.abs(row - col) <= WINDOW // 2)


def blocks_of(slots):
    for first in range(0, slots, BLOCK):
        yield first, min(max(first - WINDOW // 2, 0), slots - SPAN)


def softmax_block(q, k, allowed):
    scores = jnp.where(allowed, mat(q, k, NT) * HEAD_DIM ** (-0.5), MASKED)
    grown = jnp.exp(scores - jnp.max(scores, axis=-1, keepdims=True))
    return grown * (1.0 / jnp.sum(grown, axis=-1, keepdims=True))


def forward_kernel(nq, lens, xfull, w, cos, sin, qkv, att):
    slots = xfull.shape[0]
    proj = mat(xfull[...], w[:, : 3 * nq], NN)
    for at in range(0, 2 * nq, 128):
        piece = proj[:, at : at + 128]
        qkv[:, at : at + 128] = (piece * cos[...] + swap_halves(piece) * sin[...]).astype(BF)
    qkv[:, 2 * nq :] = proj[:, 2 * nq :].astype(BF)
    for first, start in blocks_of(slots):
        allowed = allowed_pairs(lens, first, start)
        for h in range(0, nq, HEAD_DIM):
            q = qkv[first : first + BLOCK, h : h + HEAD_DIM]
            k = qkv[start : start + SPAN, nq + h : nq + h + HEAD_DIM]
            v = qkv[start : start + SPAN, 2 * nq + h : 2 * nq + h + HEAD_DIM]
            probs = softmax_block(q, k, allowed).astype(BF)
            att[first : first + BLOCK, h : h + HEAD_DIM] = mat(probs, v, NN).astype(BF)


def backward_kernel(
    nq, lens, qkv, dbfull, att, w, cos, sin, xfull,
    dproj, grads, dqk, dv, datt,
):
    slots = xfull.shape[0]
    scale = HEAD_DIM ** (-0.5)
    datt[...] = mat(dbfull[...], w[:, 3 * nq : 4 * nq], NN).astype(BF)
    dqk[:, nq:] = jnp.zeros((slots, nq), F32)
    dv[...] = jnp.zeros((slots, nq), F32)
    for first, start in blocks_of(slots):
        allowed = allowed_pairs(lens, first, start)
        here, there = slice(first, first + BLOCK), slice(start, start + SPAN)
        for h in range(0, nq, HEAD_DIM):
            q = qkv[here, h : h + HEAD_DIM]
            k = qkv[there, nq + h : nq + h + HEAD_DIM]
            v = qkv[there, 2 * nq + h : 2 * nq + h + HEAD_DIM]
            g = datt[here, h : h + HEAD_DIM]
            p = softmax_block(q, k, allowed)
            dp = mat(g, v, NT)
            inner = jnp.sum(p * dp, axis=-1, keepdims=True)
            ds = (p * (dp - inner)).astype(BF)
            dqk[here, h : h + HEAD_DIM] = mat(ds, k, NN) * scale
            dqk[there, nq + h : nq + h + HEAD_DIM] += mat(ds, q, TN) * scale
            dv[there, h : h + HEAD_DIM] += mat(p.astype(BF), g, TN)
    for at in range(0, 2 * nq, 128):
        piece = dqk[:, at : at + 128]
        dproj[:, at : at + 128] = (piece * cos[...] - swap_halves(piece) * sin[...]).astype(BF)
    dproj[:, 2 * nq :] = dv[...].astype(BF)
    grads[:, : 3 * nq] = mat(xfull[...], dproj[...], TN).astype(BF)
    grads[:, 3 * nq :] = mat(dbfull[...], att[...], TN).astype(BF)


def gate_kernel(nf, x2full, cfull, w2, gated, dmix, grads):
    slots = x2full.shape[0]
    step = slots // 4
    for first in range(0, slots, step):
        here = slice(first, first + step)
        inputs = mat(x2full[here, :], w2[:, :nf], NN)
        gates = mat(x2full[here, :], w2[:, nf : 2 * nf], NN)
        d_gated = mat(cfull[here, :], w2[:, 2 * nf :], NN)
        below = 0.5 * (1.0 + lax.erf(inputs * 0.5**0.5))
        density = jnp.exp(-0.5 * inputs * inputs) * 0.3989422804014327
        gelu = inputs * below
        gated[here, :] = (gelu * gates).astype(BF)
        dmix[here, :nf] = ((below + inputs * density) * gates * d_gated).astype(BF)
        dmix[here, nf:] = (gelu * d_gated).astype(BF)
    grads[:, : 2 * nf] = mat(x2full[...], dmix[...], TN).astype(BF)
    grads[:, 2 * nf :] = mat(cfull[...], gated[...], TN).astype(BF)


def on_device(tokens, lengths, w_qkv, w_attn_out, w_in, w_mlp_out, gain_attn, gain_mlp, cotangent):
    dp_size, tensor_size = lax.axis_size("dp"), lax.axis_size("tensor")
    rows, width = tokens.shape
    own = w_qkv.shape[0]
    slots = rows * tensor_size
    nq, nf = w_qkv.shape[2], w_in.shape[2]
    c_attn, c_one, c_in, c_two = 3 * nq, 4 * nq, 2 * nf, 3 * nf
    gain_one = gain_attn.astype(F32)[:, None]
    gain_two = gain_mlp.astype(F32)[:, None]
    qkv_own = w_qkv.reshape(own, 3 * nq).astype(F32)
    in_own = w_in.reshape(own, 2 * nf).astype(F32)
    slab_one = jnp.concatenate([(qkv_own * gain_one).astype(BF), w_attn_out.T], axis=1)
    slab_two = jnp.concatenate([(in_own * gain_two).astype(BF), w_mlp_out.T], axis=1)
    full = jax.ShapeDtypeStruct((tensor_size, rows, width), BF)
    half = dp_size // 2
    xfull, cfull, wfull = pl.pallas_call(
        functools.partial(first_kernel, dp_size),
        out_shape=(full, full, jax.ShapeDtypeStruct((dp_size, own, c_one), BF)),
        in_specs=[VMEM, VMEM, ANY],
        out_specs=(ANY, ANY, ANY),
        scratch_shapes=[pltpu.VMEM((rows, width), BF)]
        + GATHER_SEMS * 2
        + dp_gather_sems(half),
        compiler_params=params(0),
    )(tokens, cotangent, slab_one)
    xfull = xfull.reshape(slots, width)
    cfull = cfull.reshape(slots, width)
    wfull = wfull.reshape(width, c_one)

    cos_tab, sin_tab = rope_tables(lengths, slots)
    big = pltpu.CompilerParams(vmem_limit_bytes=56 * 1024 * 1024)
    smem = pl.BlockSpec(memory_space=pltpu.SMEM)
    qkv, attended = pl.pallas_call(
        functools.partial(forward_kernel, nq),
        out_shape=(
            jax.ShapeDtypeStruct((slots, 3 * nq), BF),
            jax.ShapeDtypeStruct((slots, nq), BF),
        ),
        in_specs=[smem] + [VMEM] * 4,
        out_specs=(VMEM, VMEM),
        compiler_params=big,
    )(lengths, xfull, wfull, cos_tab, sin_tab)

    hid, x2full, w2full = pl.pallas_call(
        functools.partial(hidden_kernel, dp_size, c_attn, c_one),
        out_shape=(
            jax.ShapeDtypeStruct((rows, width), F32),
            full,
            jax.ShapeDtypeStruct((dp_size, own, c_two), BF),
        ),
        in_specs=[VMEM] * 3 + [ANY],
        out_specs=(VMEM, ANY, ANY),
        scratch_shapes=[pltpu.VMEM((rows, width), BF)]
        + GATHER_SEMS
        + scatter_scratch(rows, width)
        + dp_gather_sems(half),
        compiler_params=params(1),
    )(attended, wfull, tokens, slab_two)
    x2full = x2full.reshape(slots, width)
    w2full = w2full.reshape(width, c_two)

    gated, d_mixed, grads_two = pl.pallas_call(
        functools.partial(gate_kernel, nf),
        out_shape=(
            jax.ShapeDtypeStruct((slots, nf), BF),
            jax.ShapeDtypeStruct((slots, 2 * nf), BF),
            jax.ShapeDtypeStruct((width, c_two), BF),
        ),
        in_specs=[VMEM] * 3,
        out_specs=(VMEM,) * 3,
        compiler_params=big,
    )(x2full, cfull, w2full)

    dhid, dbfull, gsum_two = pl.pallas_call(
        functools.partial(middle_kernel, dp_size, c_in),
        out_shape=(
            jax.ShapeDtypeStruct((rows, width), F32),
            full,
            jax.ShapeDtypeStruct((own, c_two), F32),
        ),
        in_specs=[VMEM] * 5,
        out_specs=(VMEM, ANY, VMEM),
        scratch_shapes=[pltpu.VMEM((rows, width), BF)]
        + GATHER_SEMS
        + scatter_scratch(rows, width)
        + dp_scatter_scratch(half, own, c_two),
        compiler_params=params(2),
    )(d_mixed, w2full, hid, cotangent, grads_two.reshape(dp_size, own, c_two))
    dbfull = dbfull.reshape(slots, width)

    d_proj, grads_one = pl.pallas_call(
        functools.partial(backward_kernel, nq),
        out_shape=(
            jax.ShapeDtypeStruct((slots, 3 * nq), BF),
            jax.ShapeDtypeStruct((width, c_one), BF),
        ),
        in_specs=[smem] + [VMEM] * 7,
        out_specs=(VMEM, VMEM),
        scratch_shapes=[
            pltpu.VMEM((slots, 2 * nq), F32),
            pltpu.VMEM((slots, nq), F32),
            pltpu.VMEM((slots, nq), BF),
        ],
        compiler_params=big,
    )(lengths, qkv, dbfull, attended, wfull, cos_tab, sin_tab, xfull)

    others = tensor_size - 1
    grad_tokens, output, gsum_one, gains = pl.pallas_call(
        functools.partial(last_kernel, dp_size, tensor_size, c_attn, c_in),
        out_shape=(
            jax.ShapeDtypeStruct((rows, width), BF),
            jax.ShapeDtypeStruct((rows, width), BF),
            jax.ShapeDtypeStruct((own, c_one), F32),
            jax.ShapeDtypeStruct((own, 128), F32),
        ),
        in_specs=[VMEM] * 11,
        out_specs=(VMEM,) * 4,
        scratch_shapes=[
            pltpu.VMEM((own, 128), F32),
            pltpu.VMEM((others, own, 128), F32),
            pltpu.SemaphoreType.DMA((others,)),
            pltpu.SemaphoreType.DMA((others,)),
        ]
        + scatter_scratch(rows, width) * 2
        + dp_scatter_scratch(half, own, c_one),
        compiler_params=params(3),
    )(
        d_proj, wfull, tokens, dhid, grads_one.reshape(dp_size, own, c_one), gated, w2full, hid,
        qkv_own, in_own, gsum_two,
    )
    return (
        output,
        grad_tokens,
        (gsum_one[:, :c_attn] * gain_one).reshape(own, 3, nq),
        gsum_one[:, c_attn:].T,
        (gsum_two[:, :c_in] * gain_two).reshape(own, 2, nf),
        gsum_two[:, c_in:].T,
        gains[:, 0],
        gains[:, 64],
    )


def solution(mesh):
    return jax.shard_map(
        on_device,
        mesh=mesh,
        in_specs=(
            P(("dp", "tensor"), None),
            P("dp", None),
            P("dp", None, "tensor"),
            P("tensor", "dp"),
            P("dp", None, "tensor"),
            P("tensor", "dp"),
            P("dp"),
            P("dp"),
            P(("dp", "tensor"), None),
        ),
        out_specs=(
            P(("dp", "tensor"), None),
            P(("dp", "tensor"), None),
            P("dp", None, "tensor"),
            P("tensor", "dp"),
            P("dp", None, "tensor"),
            P("tensor", "dp"),
            P("dp"),
            P("dp"),
        ),
        check_vma=False,
    )
```

```python
import functools

import jax
import jax.numpy as jnp
from jax import lax
from jax.experimental import pallas as pl
from jax.experimental.pallas import tpu as pltpu
from jax.sharding import PartitionSpec as P

HEAD_DIM = 64
WINDOW = 128
NORM_EPS = 1e-05
ROPE_BASE = 10000.0
MASKED = -1e30
MESH = pl.DeviceIdType.MESH
BF = jnp.bfloat16
F32 = jnp.float32
NT = (((1,), (1,)), ((), ()))
VMEM = pl.BlockSpec(memory_space=pltpu.VMEM)
ANY = pl.BlockSpec(memory_space=pl.ANY)


def normal_rows(values):
    centre = values - jnp.mean(values, axis=-1, keepdims=True)
    spread = jnp.mean(centre * centre, axis=-1, keepdims=True)
    inv = lax.rsqrt(spread + NORM_EPS)
    return centre * inv, inv


def normal_back(values, grad):
    xhat, inv = normal_rows(values)
    mean_g = jnp.mean(grad, axis=-1, keepdims=True)
    mean_gx = jnp.mean(grad * xhat, axis=-1, keepdims=True)
    return inv * (grad - mean_g - xhat * mean_gx)


def remote(src, dst, send, recv, dev):
    return pltpu.make_async_remote_copy(
        src_ref=src, dst_ref=dst, send_sem=send, recv_sem=recv, device_id=dev, device_id_type=MESH
    )


def tensor_place():
    dp, t = lax.axis_index("dp"), lax.axis_index("tensor")
    x, core = lax.div(t, 2), lax.rem(t, 2)
    return dp, t, x, core, x * 2 + 1 - core, (1 - x) * 2 + core


def dp_place(dp_size):
    dp, t = lax.axis_index("dp"), lax.axis_index("tensor")
    return dp, t, lax.div(dp, 2), lax.rem(dp, 2), dp_size // 2


def greet(devices):
    barrier = pltpu.get_barrier_semaphore()
    for dev in devices:
        pl.semaphore_signal(barrier, inc=1, device_id=dev, device_id_type=MESH)
    pl.semaphore_wait(barrier, len(devices))


def tensor_peers():
    dp, t, x, core, corep, xp = tensor_place()
    return [(dp, corep), (dp, xp)]


def tensor_others(size):
    dp, t = lax.axis_index("dp"), lax.axis_index("tensor")
    return [(dp, lax.rem(t + k, size)) for k in range(1, size)]


def dp_peers(dp_size):
    dp, t, hi, lo, high = dp_place(dp_size)
    return [(hi * 2 + 1 - lo, t)] + [(lax.rem(hi + k, high) * 2 + lo, t) for k in range(1, high)]


PIECES = 2


def piece_rows(rows):
    step = rows // PIECES
    return [(c, pl.ds(c * step, step)) for c in range(PIECES)]


class Gather:
    def __init__(self, src, out, sems):
        dp, t, x, core, corep, xp = tensor_place()
        send, recv, here = sems
        self.own = pltpu.make_async_copy(src, out.at[t], here)
        last = 2 * PIECES
        self.to_core = remote(src, out.at[t], send.at[last], recv.at[last], (dp, corep))
        self.over_x, self.relay = [], []
        for c, cut in piece_rows(src.shape[0]):
            self.over_x.append(
                remote(src.at[cut], out.at[t, cut], send.at[c], recv.at[c], (dp, xp))
            )
            at = PIECES + c
            self.relay.append(
                remote(out.at[xp, cut], out.at[xp, cut], send.at[at], recv.at[at], (dp, corep))
            )

    def start(self):
        for copy in self.over_x:
            copy.start()
        self.to_core.start()
        self.own.start()

    def forward(self):
        for arrived, copy in zip(self.over_x, self.relay):
            arrived.wait_recv()
            copy.start()

    def finish(self):
        self.to_core.wait_recv()
        for copy in self.relay:
            copy.wait_recv()
        for copy in self.over_x + self.relay + [self.to_core]:
            copy.wait_send()
        self.own.wait()


TENSOR_COPIES = 2 * PIECES + 1
GATHER_SEMS = [
    pltpu.SemaphoreType.DMA((TENSOR_COPIES,)),
    pltpu.SemaphoreType.DMA((TENSOR_COPIES,)),
    pltpu.SemaphoreType.DMA,
]


class ScatterSum:
    def __init__(self, part, scratch):
        self.part = part
        self.sbuf, self.r1, self.pbuf, self.r2, send, recv = scratch
        dp, t, x, core, corep, xp = tensor_place()
        self.place = (t, x, core, corep, xp)
        pair = (dp, corep)
        last = 2 * PIECES
        self.near = remote(self.sbuf.at[1], self.r1.at[1], send.at[last], recv.at[last], pair)
        self.far, self.over = [], []
        self.rows = self.pbuf.shape[0]
        for c, cut in piece_rows(self.rows):
            self.far.append(
                remote(self.sbuf.at[0, cut], self.r1.at[0, cut], send.at[c], recv.at[c], pair)
            )
            at = PIECES + c
            self.over.append(
                remote(self.pbuf.at[cut], self.r2.at[cut], send.at[at], recv.at[at], (dp, xp))
            )

    def begin(self):
        t, x, core, corep, xp = self.place
        step = self.rows // PIECES
        for c in range(PIECES):
            low, high = c * step, (c + 1) * step
            self.sbuf[0, low:high] = self.part((1 - x) * 2 + 1 - core, low, step).astype(BF)
            self.far[c].start()
        for c in range(PIECES):
            low, high = c * step, (c + 1) * step
            mine = self.part(xp, low, step)
            self.far[c].wait_recv()
            self.pbuf[low:high] = (mine + self.r1[0, low:high].astype(F32)).astype(BF)
            self.over[c].start()
        self.sbuf[1] = self.part(corep, 0, self.rows).astype(BF)
        self.near.start()

    def finish(self):
        total = self.part(self.place[0], 0, self.rows)
        self.near.wait_recv()
        total = total + self.r1[1].astype(F32)
        for copy in self.over:
            copy.wait_recv()
        total = total + self.r2[...].astype(F32)
        for copy in self.far + self.over + [self.near]:
            copy.wait_send()
        return total


class DpGather:
    def __init__(self, dp_size, slab, full, sems):
        zsend, zrecv, ysend, yrecv, here = sems
        dp, t, hi, lo, high = dp_place(dp_size)
        ypeer = (hi * 2 + 1 - lo, t)
        self.mine = pltpu.make_async_copy(slab, full.at[dp], here)
        self.ycopies = [remote(slab, full.at[dp], ysend.at[0], yrecv.at[0], ypeer)]
        self.zcopies = []
        for k in range(1, high):
            peer = (lax.rem(hi + k, high) * 2 + lo, t)
            self.zcopies.append(remote(slab, full.at[dp], zsend.at[k], zrecv.at[k], peer))
            block = lax.rem(hi - k + high, high) * 2 + lo
            self.ycopies.append(
                remote(full.at[block], full.at[block], ysend.at[k], yrecv.at[k], ypeer)
            )

    def start(self):
        self.ycopies[0].start()
        for copy in self.zcopies:
            copy.start()
        self.mine.start()

    def forward(self):
        for zcopy, ycopy in zip(self.zcopies, self.ycopies[1:]):
            zcopy.wait_recv()
            ycopy.start()

    def finish(self):
        for copy in self.ycopies:
            copy.wait_recv()
        for copy in self.ycopies + self.zcopies:
            copy.wait_send()
        self.mine.wait()


class DpScatter:
    def __init__(self, dp_size, grads, scratch):
        self.grads = grads
        self.ry, self.zs, self.zr, ysend, yrecv, zsend, zrecv = scratch
        dp, t, hi, lo, high = dp_place(dp_size)
        ypeer = (hi * 2 + 1 - lo, t)
        self.high = high
        self.ycopies, self.zcopies, self.blocks = [], [], []
        for k in range(high):
            block_hi = lax.rem(hi + k, high)
            self.blocks.append(block_hi * 2 + lo)
            self.ycopies.append(
                remote(
                    grads.at[block_hi * 2 + 1 - lo], self.ry.at[k], ysend.at[k], yrecv.at[k], ypeer
                )
            )
            if k:
                peer = (block_hi * 2 + lo, t)
                self.zcopies.append(
                    remote(self.zs.at[k], self.zr.at[k], zsend.at[k], zrecv.at[k], peer)
                )

    def start(self):
        for copy in self.ycopies[1:] + self.ycopies[:1]:
            copy.start()

    def forward(self):
        for k in range(1, self.high):
            self.ycopies[k].wait_recv()
            pair_sum = self.grads[self.blocks[k]].astype(F32) + self.ry[k].astype(F32)
            self.zs[k] = pair_sum.astype(BF)
            self.zcopies[k - 1].start()

    def finish(self):
        self.ycopies[0].wait_recv()
        total = self.grads[self.blocks[0]].astype(F32) + self.ry[0].astype(F32)
        for k in range(1, self.high):
            self.zcopies[k - 1].wait_recv()
            total = total + self.zr[k].astype(F32)
        for copy in self.ycopies + self.zcopies:
            copy.wait_send()
        return total


def dp_gather_sems(half):
    return [pltpu.SemaphoreType.DMA((half,))] * 4 + [pltpu.SemaphoreType.DMA]


def dp_scatter_scratch(half, own, width):
    return [pltpu.VMEM((half, own, width), BF)] * 3 + [pltpu.SemaphoreType.DMA((half,))] * 4


def scatter_scratch(rows, width):
    return [
        pltpu.VMEM((2, rows, width), BF),
        pltpu.VMEM((2, rows, width), BF),
        pltpu.VMEM((rows, width), BF),
        pltpu.VMEM((rows, width), BF),
        pltpu.SemaphoreType.DMA((TENSOR_COPIES,)),
        pltpu.SemaphoreType.DMA((TENSOR_COPIES,)),
    ]


def params(ident):
    return pltpu.CompilerParams(
        collective_id=ident, has_side_effects=True, vmem_limit_bytes=48 * 1024 * 1024
    )


def block_product(lhs_ref, w, low, high, rows):
    def part(b, first, count):
        lhs = lhs_ref[pl.ds(pl.multiple_of(b * rows + first, 128), count), :]
        return lax.dot_general(lhs, w[:, low:high], NT, preferred_element_type=F32)

    return part


def first_kernel(dp_size, tok, cot, slab, xfull, cfull, wfull, xhat, *scr):
    gx, gc = Gather(xhat, xfull, scr[0:3]), Gather(cot, cfull, scr[3:6])
    weights = DpGather(dp_size, slab, wfull, scr[6:11])
    greet(tensor_peers() + dp_peers(dp_size))
    weights.start()
    xhat[...] = normal_rows(tok[...].astype(F32))[0].astype(BF)
    gx.start()
    gc.start()
    weights.forward()
    gx.forward()
    gc.forward()
    gx.finish()
    gc.finish()
    weights.finish()


def hidden_kernel(dp_size, c_attn, c_one, att, w, tok, slab, hid, x2full, w2full, xhat, *scr):
    rows = tok.shape[0]
    greet(tensor_peers() + dp_peers(dp_size))
    weights = DpGather(dp_size, slab, w2full, scr[9:14])
    weights.start()
    branch = ScatterSum(block_product(att, w, c_attn, c_one, rows), scr[3:9])
    branch.begin()
    hidden = tok[...].astype(F32) + branch.finish()
    hid[...] = hidden
    xhat[...] = normal_rows(hidden)[0].astype(BF)
    gather = Gather(xhat, x2full, scr[0:3])
    gather.start()
    weights.forward()
    gather.forward()
    gather.finish()
    weights.finish()


def middle_kernel(dp_size, c_in, dmix, w2, hid, cot, grads, dhid, dbfull, gsum, dbr, *scr):
    rows = hid.shape[0]
    greet(tensor_peers() + dp_peers(dp_size))
    weight_sum = DpScatter(dp_size, grads, scr[9:16])
    weight_sum.start()
    normed = ScatterSum(block_product(dmix, w2, 0, c_in, rows), scr[3:9])
    normed.begin()
    weight_sum.forward()
    d_hidden = cot[...].astype(F32) + normal_back(hid[...], normed.finish())
    dhid[...] = d_hidden
    dbr[...] = d_hidden.astype(BF)
    gather = Gather(dbr, dbfull, scr[0:3])
    gather.start()
    gather.forward()
    gsum[...] = weight_sum.finish()
    gather.finish()


def last_kernel(
    dp_size, t_size, c_attn, c_in, dproj, w, tok, dhid, grads, gated, w2, hid, raw_one, raw_two,
    gsum_two, gtok, out, gsum, gains, gbuf, grecv, gsend_sem, grecv_sem, *scr,
):
    rows = tok.shape[0]
    others = tensor_others(t_size)
    greet(others + dp_peers(dp_size))
    weight_sum = DpScatter(dp_size, grads, scr[12:19])
    weight_sum.start()
    normed = ScatterSum(block_product(dproj, w, 0, c_attn, rows), scr[0:6])
    result = ScatterSum(block_product(gated, w2, c_in, w2.shape[1], rows), scr[6:12])
    normed.begin()
    weight_sum.forward()
    result.begin()
    gtok[...] = (dhid[...] + normal_back(tok[...].astype(F32), normed.finish())).astype(BF)
    total = weight_sum.finish()
    gsum[...] = total
    gain_one = jnp.sum(total[:, :c_attn] * raw_one[...], axis=1, keepdims=True)
    gain_two = jnp.sum(gsum_two[:, :c_in] * raw_two[...], axis=1, keepdims=True)
    lane = lax.broadcasted_iota(jnp.int32, gbuf.shape, 1)
    gbuf[...] = jnp.where(lane < 64, gain_one, gain_two)
    copies = [
        remote(gbuf, grecv.at[k], gsend_sem.at[k], grecv_sem.at[k], peer)
        for k, peer in enumerate(others)
    ]
    for copy in copies:
        copy.start()
    out[...] = (hid[...] + result.finish()).astype(BF)
    gain_total = gbuf[...]
    for k, copy in enumerate(copies):
        copy.wait_recv()
        gain_total = gain_total + grecv[k]
    gains[...] = gain_total
    for copy in copies:
        copy.wait_send()


BLOCK = 128
SPAN = BLOCK + WINDOW
NN = (((1,), (0,)), ((), ()))
TN = (((0,), (0,)), ((), ()))


def mat(left, right, dims):
    return lax.dot_general(left, right, dims, preferred_element_type=F32)


def rope_tables(lengths, slots):
    slot_ids = jnp.arange(slots, dtype=jnp.int32)
    first_end, second_end = lengths[0, 0], lengths[0, 0] + lengths[0, 1]
    start = jnp.where(
        slot_ids < first_end, 0, jnp.where(slot_ids < second_end, first_end, second_end)
    )
    half = HEAD_DIM // 2
    inv_freq = ROPE_BASE ** (-(jnp.arange(half, dtype=F32) * 2.0) / HEAD_DIM)
    angles = inv_freq[:, None] * (slot_ids - start).astype(F32)[None, :]
    return jnp.cos(angles), jnp.sin(angles)


def two_heads(cos, sin):
    cos_part, sin_part = cos[...], sin[...]
    return (
        jnp.concatenate([cos_part] * 4, axis=0).T,
        jnp.concatenate([-sin_part, sin_part] * 2, axis=0).T,
    )


def swap_halves(values):
    half = HEAD_DIM // 2
    lane = lax.broadcasted_iota(jnp.int32, values.shape, 1)
    ahead = pltpu.roll(values, 2 * HEAD_DIM - half, 1)
    behind = pltpu.roll(values, half, 1)
    return jnp.where(lax.rem(lane, HEAD_DIM) < half, ahead, behind)


def allowed_pairs(lens, first, start):
    row = first + lax.broadcasted_iota(jnp.int32, (BLOCK, SPAN), 0)
    col = start + lax.broadcasted_iota(jnp.int32, (BLOCK, SPAN), 1)
    one, two = lens[0, 0], lens[0, 0] + lens[0, 1]
    ids = lambda v: (v >= one).astype(jnp.int32) + (v >= two).astype(jnp.int32)
    return (ids(row) == ids(col)) & (jnp.abs(row - col) <= WINDOW // 2)


def blocks_of(slots):
    for first in range(0, slots, BLOCK):
        yield first, min(max(first - WINDOW // 2, 0), slots - SPAN)


def softmax_block(q, k, allowed):
    scores = jnp.where(allowed, mat(q, k, NT) * HEAD_DIM ** (-0.5), MASKED)
    grown = jnp.exp(scores - jnp.max(scores, axis=-1, keepdims=True))
    return grown * (1.0 / jnp.sum(grown, axis=-1, keepdims=True))


def forward_kernel(nq, lens, xfull, w, cos, sin, qkv, att):
    slots = xfull.shape[0]
    cos_tab, sin_tab = two_heads(cos, sin)
    proj = mat(xfull[...], w[:, : 3 * nq], NN)
    for at in range(0, 2 * nq, 128):
        piece = proj[:, at : at + 128]
        qkv[:, at : at + 128] = (piece * cos_tab + swap_halves(piece) * sin_tab).astype(BF)
    qkv[:, 2 * nq :] = proj[:, 2 * nq :].astype(BF)
    for first, start in blocks_of(slots):
        allowed = allowed_pairs(lens, first, start)
        for h in range(0, nq, HEAD_DIM):
            q = qkv[first : first + BLOCK, h : h + HEAD_DIM]
            k = qkv[start : start + SPAN, nq + h : nq + h + HEAD_DIM]
            v = qkv[start : start + SPAN, 2 * nq + h : 2 * nq + h + HEAD_DIM]
            probs = softmax_block(q, k, allowed).astype(BF)
            att[first : first + BLOCK, h : h + HEAD_DIM] = mat(probs, v, NN).astype(BF)


def backward_kernel(
    nq, lens, qkv, dbfull, att, w, cos, sin, xfull,
    dproj, grads, dqk, dv, datt,
):
    slots = xfull.shape[0]
    scale = HEAD_DIM ** (-0.5)
    datt[...] = mat(dbfull[...], w[:, 3 * nq : 4 * nq], NN).astype(BF)
    dqk[:, nq:] = jnp.zeros((slots, nq), F32)
    dv[...] = jnp.zeros((slots, nq), F32)
    for first, start in blocks_of(slots):
        allowed = allowed_pairs(lens, first, start)
        here, there = slice(first, first + BLOCK), slice(start, start + SPAN)
        for h in range(0, nq, HEAD_DIM):
            q = qkv[here, h : h + HEAD_DIM]
            k = qkv[there, nq + h : nq + h + HEAD_DIM]
            v = qkv[there, 2 * nq + h : 2 * nq + h + HEAD_DIM]
            g = datt[here, h : h + HEAD_DIM]
            p = softmax_block(q, k, allowed)
            dp = mat(g, v, NT)
            inner = jnp.sum(p * dp, axis=-1, keepdims=True)
            ds = (p * (dp - inner)).astype(BF)
            dqk[here, h : h + HEAD_DIM] = mat(ds, k, NN) * scale
            dqk[there, nq + h : nq + h + HEAD_DIM] += mat(ds, q, TN) * scale
            dv[there, h : h + HEAD_DIM] += mat(p.astype(BF), g, TN)
    cos_tab, sin_tab = two_heads(cos, sin)
    for at in range(0, 2 * nq, 128):
        piece = dqk[:, at : at + 128]
        dproj[:, at : at + 128] = (piece * cos_tab - swap_halves(piece) * sin_tab).astype(BF)
    dproj[:, 2 * nq :] = dv[...].astype(BF)
    grads[:, : 3 * nq] = mat(xfull[...], dproj[...], TN).astype(BF)
    grads[:, 3 * nq :] = mat(dbfull[...], att[...], TN).astype(BF)


def gate_kernel(nf, x2full, cfull, w2, gated, dmix, grads):
    slots = x2full.shape[0]
    step = slots // 4
    for first in range(0, slots, step):
        here = slice(first, first + step)
        inputs = mat(x2full[here, :], w2[:, :nf], NN)
        gates = mat(x2full[here, :], w2[:, nf : 2 * nf], NN)
        d_gated = mat(cfull[here, :], w2[:, 2 * nf :], NN)
        below = 0.5 * (1.0 + lax.erf(inputs * 0.5**0.5))
        density = jnp.exp(-0.5 * inputs * inputs) * 0.3989422804014327
        gelu = inputs * below
        gated[here, :] = (gelu * gates).astype(BF)
        dmix[here, :nf] = ((below + inputs * density) * gates * d_gated).astype(BF)
        dmix[here, nf:] = (gelu * d_gated).astype(BF)
    grads[:, : 2 * nf] = mat(x2full[...], dmix[...], TN).astype(BF)
    grads[:, 2 * nf :] = mat(cfull[...], gated[...], TN).astype(BF)


def on_device(tokens, lengths, w_qkv, w_attn_out, w_in, w_mlp_out, gain_attn, gain_mlp, cotangent):
    dp_size, tensor_size = lax.axis_size("dp"), lax.axis_size("tensor")
    rows, width = tokens.shape
    own = w_qkv.shape[0]
    slots = rows * tensor_size
    nq, nf = w_qkv.shape[2], w_in.shape[2]
    c_attn, c_one, c_in, c_two = 3 * nq, 4 * nq, 2 * nf, 3 * nf
    gain_one = gain_attn.astype(F32)[:, None]
    gain_two = gain_mlp.astype(F32)[:, None]
    qkv_own = w_qkv.reshape(own, 3 * nq).astype(F32)
    in_own = w_in.reshape(own, 2 * nf).astype(F32)
    slab_one = jnp.concatenate([(qkv_own * gain_one).astype(BF), w_attn_out.T], axis=1)
    slab_two = jnp.concatenate([(in_own * gain_two).astype(BF), w_mlp_out.T], axis=1)
    full = jax.ShapeDtypeStruct((tensor_size, rows, width), BF)
    half = dp_size // 2
    xfull, cfull, wfull = pl.pallas_call(
        functools.partial(first_kernel, dp_size),
        out_shape=(full, full, jax.ShapeDtypeStruct((dp_size, own, c_one), BF)),
        in_specs=[VMEM, VMEM, ANY],
        out_specs=(ANY, ANY, ANY),
        scratch_shapes=[pltpu.VMEM((rows, width), BF)]
        + GATHER_SEMS * 2
        + dp_gather_sems(half),
        compiler_params=params(0),
    )(tokens, cotangent, slab_one)
    xfull = xfull.reshape(slots, width)
    cfull = cfull.reshape(slots, width)
    wfull = wfull.reshape(width, c_one)

    cos_tab, sin_tab = rope_tables(lengths, slots)
    big = pltpu.CompilerParams(vmem_limit_bytes=56 * 1024 * 1024)
    smem = pl.BlockSpec(memory_space=pltpu.SMEM)
    qkv, attended = pl.pallas_call(
        functools.partial(forward_kernel, nq),
        out_shape=(
            jax.ShapeDtypeStruct((slots, 3 * nq), BF),
            jax.ShapeDtypeStruct((slots, nq), BF),
        ),
        in_specs=[smem] + [VMEM] * 4,
        out_specs=(VMEM, VMEM),
        compiler_params=big,
    )(lengths, xfull, wfull, cos_tab, sin_tab)

    hid, x2full, w2full = pl.pallas_call(
        functools.partial(hidden_kernel, dp_size, c_attn, c_one),
        out_shape=(
            jax.ShapeDtypeStruct((rows, width), F32),
            full,
            jax.ShapeDtypeStruct((dp_size, own, c_two), BF),
        ),
        in_specs=[VMEM] * 3 + [ANY],
        out_specs=(VMEM, ANY, ANY),
        scratch_shapes=[pltpu.VMEM((rows, width), BF)]
        + GATHER_SEMS
        + scatter_scratch(rows, width)
        + dp_gather_sems(half),
        compiler_params=params(1),
    )(attended, wfull, tokens, slab_two)
    x2full = x2full.reshape(slots, width)
    w2full = w2full.reshape(width, c_two)

    gated, d_mixed, grads_two = pl.pallas_call(
        functools.partial(gate_kernel, nf),
        out_shape=(
            jax.ShapeDtypeStruct((slots, nf), BF),
            jax.ShapeDtypeStruct((slots, 2 * nf), BF),
            jax.ShapeDtypeStruct((width, c_two), BF),
        ),
        in_specs=[VMEM] * 3,
        out_specs=(VMEM,) * 3,
        compiler_params=big,
    )(x2full, cfull, w2full)

    dhid, dbfull, gsum_two = pl.pallas_call(
        functools.partial(middle_kernel, dp_size, c_in),
        out_shape=(
            jax.ShapeDtypeStruct((rows, width), F32),
            full,
            jax.ShapeDtypeStruct((own, c_two), F32),
        ),
        in_specs=[VMEM] * 5,
        out_specs=(VMEM, ANY, VMEM),
        scratch_shapes=[pltpu.VMEM((rows, width), BF)]
        + GATHER_SEMS
        + scatter_scratch(rows, width)
        + dp_scatter_scratch(half, own, c_two),
        compiler_params=params(2),
    )(d_mixed, w2full, hid, cotangent, grads_two.reshape(dp_size, own, c_two))
    dbfull = dbfull.reshape(slots, width)

    d_proj, grads_one = pl.pallas_call(
        functools.partial(backward_kernel, nq),
        out_shape=(
            jax.ShapeDtypeStruct((slots, 3 * nq), BF),
            jax.ShapeDtypeStruct((width, c_one), BF),
        ),
        in_specs=[smem] + [VMEM] * 7,
        out_specs=(VMEM, VMEM),
        scratch_shapes=[
            pltpu.VMEM((slots, 2 * nq), F32),
            pltpu.VMEM((slots, nq), F32),
            pltpu.VMEM((slots, nq), BF),
        ],
        compiler_params=big,
    )(lengths, qkv, dbfull, attended, wfull, cos_tab, sin_tab, xfull)

    others = tensor_size - 1
    grad_tokens, output, gsum_one, gains = pl.pallas_call(
        functools.partial(last_kernel, dp_size, tensor_size, c_attn, c_in),
        out_shape=(
            jax.ShapeDtypeStruct((rows, width), BF),
            jax.ShapeDtypeStruct((rows, width), BF),
            jax.ShapeDtypeStruct((own, c_one), F32),
            jax.ShapeDtypeStruct((own, 128), F32),
        ),
        in_specs=[VMEM] * 11,
        out_specs=(VMEM,) * 4,
        scratch_shapes=[
            pltpu.VMEM((own, 128), F32),
            pltpu.VMEM((others, own, 128), F32),
            pltpu.SemaphoreType.DMA((others,)),
            pltpu.SemaphoreType.DMA((others,)),
        ]
        + scatter_scratch(rows, width) * 2
        + dp_scatter_scratch(half, own, c_one),
        compiler_params=params(3),
    )(
        d_proj, wfull, tokens, dhid, grads_one.reshape(dp_size, own, c_one), gated, w2full, hid,
        qkv_own, in_own, gsum_two,
    )
    return (
        output,
        grad_tokens,
        (gsum_one[:, :c_attn] * gain_one).reshape(own, 3, nq),
        gsum_one[:, c_attn:].T,
        (gsum_two[:, :c_in] * gain_two).reshape(own, 2, nf),
        gsum_two[:, c_in:].T,
        gains[:, 0],
        gains[:, 64],
    )


def solution(mesh):
    return jax.shard_map(
        on_device,
        mesh=mesh,
        in_specs=(
            P(("dp", "tensor"), None),
            P("dp", None),
            P("dp", None, "tensor"),
            P("tensor", "dp"),
            P("dp", None, "tensor"),
            P("tensor", "dp"),
            P("dp"),
            P("dp"),
            P(("dp", "tensor"), None),
        ),
        out_specs=(
            P(("dp", "tensor"), None),
            P(("dp", "tensor"), None),
            P("dp", None, "tensor"),
            P("tensor", "dp"),
            P("dp", None, "tensor"),
            P("tensor", "dp"),
            P("dp"),
            P("dp"),
        ),
        check_vma=False,
    )
```
